256 devices in a mesh: pipe: 4 (over x), expert: 64 (over z, y, core).
Axes of the slice: x: 4, y: 4, z: 8, core: 2. Of those that a mesh axis runs over, the one named last changes fastest.
Arguments:
- fwd_input: bfloat16 [4, 1024, 3584], P('pipe', 'expert'), may hold values from -6 to 6
- fwd_routes: int32 [4, 1024, 8], P('pipe', 'expert'), may hold values from 0 to 31, all different within a row; in each aligned block of 16 rows (0 to 15, 16 to 31, ..., all dimensions but the last counted through in order) at most 6 rows name the same one
- fwd_weight: float32 [4, 1024, 8], P('pipe', 'expert'), may hold values from 0.1 to 1
- bwd_input: bfloat16 [4, 1024, 3584], P('pipe', 'expert'), may hold values from -6 to 6
- bwd_grad: bfloat16 [4, 1024, 3584], P('pipe', 'expert'), may hold values from -6 to 6
- bwd_routes: int32 [4, 1024, 8], P('pipe', 'expert'), may hold values from 0 to 31, all different within a row; in each aligned block of 16 rows (0 to 15, 16 to 31, ..., all dimensions but the last counted through in order) at most 6 rows name the same one
- bwd_weight: float32 [4, 1024, 8], P('pipe', 'expert'), may hold values from 0.1 to 1
- w_gate: bfloat16 [4, 64, 3584, 512], P('pipe', 'expert'), may hold values from -0.09375 to 0.09375
- w_up: bfloat16 [4, 64, 3584, 512], P('pipe', 'expert'), may hold values from -0.09375 to 0.09375
- w_down: bfloat16 [4, 64, 512, 3584], P('pipe', 'expert'), may hold values from -0.1875 to 0.1875
Outputs:
- fwd_next: bfloat16 [4, 1024, 3584], P('pipe', 'expert')
- grad_prev: bfloat16 [4, 1024, 3584], P('pipe', 'expert')
The draws below stay inside these ranges and needn't reach their ends.
Inputs may be any that keep to these rules, and one draw needn't show every extreme that they name: `fwd_routes`: the 16 tokens of one device name one expert at most 6 times; in every draw some expert is named exactly 6 times by one device's tokens. A token's 8 experts differ. `bwd_routes`: as for fwd_routes.
All inputs are finite; a program needn't handle non-finite values.
Results may differ from the reference program's by a relative error of at most 0.0058.
Values may be sent and summed in bfloat16 or wider, within the bound.
A program may use at most 128 MiB of HBM per device.

```python
import math
import jax
import jax.numpy as jnp
import numpy as np
from jax import lax

D = 3584
FF_WIN = 1024
SPLIT = 2
E = 32
TOP = 8
TOK_DEV = 16
FF_DEV = 512
CAP = 6
TOKENS = 1024
UNITS = 64
N_PIPE = 4
N_EXPERT = 64


def steps_of(stream_key, shape, cuts, smallest, top_value):
    loudness, own = 1.0, jax.random.fold_in(stream_key, 6)
    for dim, shards_of in cuts:
        heights = jnp.exp(jax.random.uniform(jax.random.fold_in(own, dim), (shards_of,), jnp.float32, smallest / len(cuts), top_value / len(cuts)))
        loudness = loudness * jnp.repeat(heights, shape[dim] // shards_of).reshape([-1 if axis == dim else 1 for axis in range(len(shape))])
    return loudness


def deal_out(key, own, number, rows, count, top, most, slope):
    order = jax.random.permutation(key, count)
    packed, usual = load_shares(count, rows * top, most, slope, True), load_shares(count, rows * top, most, slope, False)
    places = jnp.arange(count)

    def named(lengths, offset_by):
        used = int((lengths > 0).sum())
        fixed = max(1, used // 4)
        moved = fixed + (places - fixed + offset_by * (used - fixed)) % max(1, count - fixed)
        return jnp.zeros((count,), jnp.int32).at[order[jnp.where(places < fixed, places, moved)]].set(jnp.asarray(lengths, jnp.int32))

    lengths = jnp.where(number % 4 == 0, named(packed, number // 4), named(usual, number - number // 4 - 1))
    mixed = jax.random.permutation(jax.random.fold_in(own, 3), count)
    source_of, receiver = mixed[0:count // 2 * 2:2], mixed[1:count // 2 * 2:2]
    room = jnp.minimum(lengths[source_of] - 1, most - lengths[receiver]) // 2
    room = jnp.where((source_of == order[0]) | (receiver == order[0]) | (lengths[receiver] == 0), 0, jnp.maximum(room, 0))
    moved = jax.random.randint(jax.random.fold_in(own, 4), (count // 2,), 0, 1 << 20) % (room + 1)
    lengths = lengths.at[source_of].add(-moved).at[receiver].add(moved)
    items = jnp.searchsorted(jnp.cumsum(lengths), jnp.arange(rows * top), side="right").astype(jnp.int32)
    listing = items.reshape(top, rows).T
    listing = listing[jax.random.permutation(jax.random.fold_in(own, 1), rows)]
    offset_by = jax.random.randint(jax.random.fold_in(own, 2), (rows, 1), 0, top)
    return jnp.take_along_axis(listing, (jnp.arange(top)[None, :] + offset_by) % top, axis=1)


def load_shares(count, total, bound, lean, full):
    portions = [(1 << 20) // math.isqrt(grade ** lean) + 1 for grade in range(1, count + 1)]
    largest = bound if full else min(bound, max(-(-total // count), total * portions[0] // sum(portions)))
    least = 1 if total - largest >= count - 1 else 0
    holding, rest = [largest] + [least] * (count - 1), total - largest - least * (count - 1)
    while rest > 0:
        candidates = [i for i in range(1, count) if holding[i] < largest] or [i for i in range(1, count) if holding[i] < bound]
        mass, remaining = sum([portions[i] for i in candidates]), rest
        for i in candidates:
            addition = min(bound - holding[i], max(1, remaining * portions[i] // mass), rest)
            holding[i] = holding[i] + addition
            rest = rest - addition
    return np.array(holding)


def bell_draw(key, shape, width, bound, shards=(), kind=jnp.bfloat16):
    factor_of = steps_of(key, shape, shards, -0.22, 0.18) if shards else 1.0
    array = jax.random.normal(key, shape, jnp.float32) * width * factor_of
    return jnp.minimum(jnp.maximum(array, -bound), bound).astype(kind)


def setup_inputs(seed: int = 0) -> dict:
    key_of = jax.random.split(jax.random.key(seed), 11)
    fwd_input = bell_draw(key_of[0], (N_PIPE, TOKENS, D), 1.0, 6.0, ((0, 4), (1, 64)))
    fwd_routes_keys = jax.random.split(jax.random.fold_in(key_of[1], 1), N_PIPE * TOKENS // TOK_DEV)
    fwd_routes_turns = jax.random.permutation(jax.random.fold_in(key_of[1], 3), N_PIPE * TOKENS // TOK_DEV)
    fwd_routes = jax.vmap(lambda own, number: deal_out(jax.random.fold_in(key_of[1], 2), own, number, TOK_DEV, E, TOP, CAP, 2))(fwd_routes_keys, fwd_routes_turns).reshape((N_PIPE, TOKENS, TOP))
    fwd_weight = jnp.clip(jnp.exp(math.log(1.0) - 2.3025851 * jax.random.uniform(key_of[2], (N_PIPE, TOKENS, TOP), jnp.float32) ** steps_of(key_of[2], (N_PIPE, TOKENS, TOP), ((0, 4), (1, 64)), -0.2, 0.2)), 0.1, 1.0)
    bwd_input = bell_draw(key_of[3], (N_PIPE, TOKENS, D), 1.0, 6.0, ((0, 4), (1, 64)))
    bwd_grad = bell_draw(key_of[4], (N_PIPE, TOKENS, D), 1.0, 6.0, ((0, 4), (1, 64)))
    bwd_routes_keys = jax.random.split(jax.random.fold_in(key_of[5], 1), N_PIPE * TOKENS // TOK_DEV)
    bwd_routes_turns = jax.random.permutation(jax.random.fold_in(key_of[5], 3), N_PIPE * TOKENS // TOK_DEV)
    bwd_routes = jax.vmap(lambda own, number: deal_out(jax.random.fold_in(key_of[5], 2), own, number, TOK_DEV, E, TOP, CAP, 2))(bwd_routes_keys, bwd_routes_turns).reshape((N_PIPE, TOKENS, TOP))
    bwd_weight = jnp.clip(jnp.exp(math.log(1.0) - 2.3025851 * jax.random.uniform(key_of[6], (N_PIPE, TOKENS, TOP), jnp.float32) ** steps_of(key_of[6], (N_PIPE, TOKENS, TOP), ((0, 4), (1, 64)), -0.2, 0.2)), 0.1, 1.0)
    w_gate = bell_draw(key_of[7], (N_PIPE, UNITS, D, FF_DEV), D ** -0.5, 0.09375, ((0, 4), (1, 64)))
    w_up = bell_draw(key_of[8], (N_PIPE, UNITS, D, FF_DEV), D ** -0.5, 0.09375, ((0, 4), (1, 64)))
    w_down = bell_draw(key_of[9], (N_PIPE, UNITS, FF_DEV, D), FF_WIN ** -0.5, 0.1875, ((0, 4), (1, 64)))
    return dict(fwd_input=fwd_input, fwd_routes=fwd_routes, fwd_weight=fwd_weight, bwd_input=bwd_input, bwd_grad=bwd_grad, bwd_routes=bwd_routes, bwd_weight=bwd_weight, w_gate=w_gate, w_up=w_up, w_down=w_down)


def select_rows(routes, weights, expert):
    matched = routes == expert
    is_hit = jnp.any(matched, axis=1)
    shares = jnp.sum(jnp.where(matched, weights, 0.0), axis=1)
    position = jnp.cumsum(is_hit.astype(jnp.int32)) - 1
    row_total = N_EXPERT * CAP
    target = jnp.where(is_hit, position, row_total).astype(jnp.int32)
    row_index = jnp.zeros((row_total,), jnp.int32).at[target].set(jnp.arange(TOKENS, dtype=jnp.int32), mode="drop")
    is_valid = jnp.zeros((row_total,), weights.dtype).at[target].set(1.0, mode="drop")
    return row_index, is_valid * shares[row_index]


def section_forward(tokens, routes, weights, gate_w, up_w, down_w):
    def add_expert(totals, expert):
        row_index, scale = select_rows(routes, weights, expert)
        row_block = tokens[row_index]
        partial_value = jnp.zeros((row_block.shape[0], tokens.shape[1]), jnp.float32)
        for block_idx in range(SPLIT):
            unit_idx = expert * SPLIT + block_idx
            gate_val = jnp.dot(row_block, gate_w[unit_idx], preferred_element_type=jnp.float32)
            up_val = jnp.dot(row_block, up_w[unit_idx], preferred_element_type=jnp.float32)
            hidden = (jax.nn.silu(gate_val) * up_val).astype(jnp.bfloat16)
            partial_value = partial_value + jnp.dot(hidden, down_w[unit_idx], preferred_element_type=jnp.float32)
        rounded = lax.optimization_barrier(partial_value.astype(jnp.bfloat16)).astype(jnp.float32)
        totals = totals.at[row_index].add(scale[:, None] * rounded)
        return totals, None

    totals, _ = lax.scan(add_expert, jnp.zeros((TOKENS, tokens.shape[1]), jnp.float32), jnp.arange(E, dtype=jnp.int32))
    return totals.astype(jnp.bfloat16)


def section_backward(tokens, grads, routes, weights, gate_w, up_w, down_w):
    def add_expert(totals, expert):
        row_index, scale = select_rows(routes, weights, expert)
        row_block = tokens[row_index]
        grad_block = grads[row_index]
        partial_value = jnp.zeros((row_block.shape[0], tokens.shape[1]), jnp.float32)
        for block_idx in range(SPLIT):
            unit_idx = expert * SPLIT + block_idx
            gate_val = jnp.dot(row_block, gate_w[unit_idx], preferred_element_type=jnp.float32)
            up_val = jnp.dot(row_block, up_w[unit_idx], preferred_element_type=jnp.float32)
            sigma = jax.nn.sigmoid(gate_val)
            hid_grad = jnp.dot(grad_block, down_w[unit_idx].T, preferred_element_type=jnp.float32)
            gate_grad = (hid_grad * up_val * sigma * (1.0 + gate_val * (1.0 - sigma))).astype(jnp.bfloat16)
            up_grad = (hid_grad * gate_val * sigma).astype(jnp.bfloat16)
            partial_value = partial_value + jnp.dot(gate_grad, gate_w[unit_idx].T, preferred_element_type=jnp.float32)
            partial_value = partial_value + jnp.dot(up_grad, up_w[unit_idx].T, preferred_element_type=jnp.float32)
        rounded = lax.optimization_barrier(partial_value.astype(jnp.bfloat16)).astype(jnp.float32)
        totals = totals.at[row_index].add(scale[:, None] * rounded)
        return totals, None

    totals, _ = lax.scan(add_expert, jnp.zeros((TOKENS, tokens.shape[1]), jnp.float32), jnp.arange(E, dtype=jnp.int32))
    return totals.astype(jnp.bfloat16)


def reference(fwd_input, fwd_routes, fwd_weight, bwd_input, bwd_grad, bwd_routes, bwd_weight, w_gate, w_up, w_down):
    outputs = []
    gradients = []
    for section_idx in range(N_PIPE):
        outputs.append(section_forward(fwd_input[section_idx], fwd_routes[section_idx], fwd_weight[section_idx], w_gate[section_idx], w_up[section_idx], w_down[section_idx]))
        gradients.append(section_backward(bwd_input[section_idx], bwd_grad[section_idx], bwd_routes[section_idx], bwd_weight[section_idx], w_gate[section_idx], w_up[section_idx], w_down[section_idx]))
    empty = jnp.zeros_like(outputs[0])
    fwd_next = jnp.stack([empty] + outputs[:-1])
    grad_prev = jnp.stack(gradients[1:] + [empty])
    return fwd_next, grad_prev
```

```python
import functools

import jax
import jax.numpy as jnp
from jax import lax
from jax.experimental import pallas as pl
from jax.experimental.pallas import tpu as pltpu
from jax.sharding import PartitionSpec as P

MESH = pl.DeviceIdType.MESH
BF = jnp.bfloat16
F32 = jnp.float32

D = 3584
FF = 512
TOK = 16
CAP = 6
E = 32
TOP = 8
NX = 4
NZ = 8
NY = 4
SLOT = NZ * CAP
PLANE = NY * SLOT
ROWS = 2 * PLANE
GROUP = NZ * TOK
TILE = 256

HEAD = ((0, 512), (512, 1024), (1536, 1024), (2560, 1024))
TAIL = ((0, 1024), (1024, 1024), (2048, 1024), (3072, 512))
NH = len(HEAD)
NT = len(TAIL)
X, G, F = 0, 1, 2
B, O = 0, 1


def dot(a, b):
    return jnp.dot(a, b, preferred_element_type=F32)


def dot_nt(a, b):
    return lax.dot_general(a, b, (((1,), (1,)), ((), ())), preferred_element_type=F32)


def slots_and_shares(routes, weights):
    expert = lax.broadcasted_iota(jnp.int32, (TOK, 128), 1) & (E - 1)
    hit = jnp.zeros((TOK, 128), F32)
    share = jnp.zeros((TOK, 128), F32)
    for k in range(TOP):
        same = routes[:, k : k + 1] == expert
        hit = hit + jnp.where(same, 1.0, 0.0)
        share = share + jnp.where(same, weights[:, k : k + 1], 0.0)
    rows = lax.broadcasted_iota(jnp.int32, (TOK, TOK), 0)
    cols = lax.broadcasted_iota(jnp.int32, (TOK, TOK), 1)
    before = dot(jnp.where(rows > cols, 1.0, 0.0).astype(BF), hit.astype(BF))
    return jnp.where(hit > 0.5, before, -1.0), share


def kernel(
    xf, rf, wf, xb, gb, rb, wb, wg_h, wu_h, wd_h,
    out_f, out_b,
    wg, wu, wd, meta, onehot, mix_hi, mix_lo, ag, send, recv,
    gate, up, hid_a, hid_b, own, sib_s, sib_r, ret_s, ret_r, part, rs_s, rs_r, xs, xr,
    w_sem, m_ss, m_rs, z_ss, z_rs, y_ss, y_rs, d_ss, d_rs,
    p_ss, p_rs, r_ss, r_rs, c_ss, c_rs, x_ss, x_rs,
):
    px = lax.axis_index("pipe")
    e = lax.axis_index("expert")
    c = lax.rem(e, 2)
    y = lax.rem(lax.div(e, 2), NY)
    z = lax.div(e, 2 * NY)
    turn = 1 - 2 * c

    def at(qx, qz, qy, qc):
        return (lax.rem(qx + NX, NX), (lax.rem(qz + NZ, NZ) * NY + lax.rem(qy + NY, NY)) * 2 + qc)

    ahead = at(px, z + turn, y, c)
    behind = at(px, z - turn, y, c)
    ups = [None] + [at(px, z, y + i, c) for i in range(1, NY)]
    downs = [None] + [at(px, z, y - i, c) for i in range(1, NY)]
    sibling = at(px, z, y, 1 - c)
    x_next = at(px + 1, z, y, c)
    x_prev = at(px - 1, z, y, c)

    def remote(src, dst, ss, rs, device):
        return pltpu.make_async_remote_copy(
            src_ref=src, dst_ref=dst, send_sem=ss, recv_sem=rs, device_id=device, device_id_type=MESH
        )

    def take(ref, rs, device):
        remote(ref, ref, rs, rs, device).wait_recv()

    def sent(ref, ss, device):
        remote(ref, ref, ss, ss, device).wait_send()

    weight_copies = [
        pltpu.make_async_copy(a, b, w_sem.at[i])
        for i, (a, b) in enumerate(((wg_h, wg), (wu_h, wu), (wd_h, wd)))
    ]
    for copy in weight_copies:
        copy.start()

    barrier = pltpu.get_barrier_semaphore()
    partners = [ahead, behind, ups[1], ups[2], ups[3], sibling, x_next, x_prev]
    for device in partners:
        pl.semaphore_signal(barrier, inc=1, device_id=device, device_id_type=MESH)

    lane = lax.broadcasted_iota(jnp.int32, (TOK, 128), 1)
    pos_f, share_f = slots_and_shares(rf[...], wf[...])
    pos_b, share_b = slots_and_shares(rb[...], wb[...])
    meta[0:TOK, :] = jnp.where(
        lane < E, pos_f, jnp.where(lane < 2 * E, share_f, jnp.where(lane < 3 * E, pos_b, share_b))
    )
    pl.semaphore_wait(barrier, len(partners))

    def rows(block):
        return pl.ds(block * TOK, TOK)

    def meta_hop(src, dst, device):
        remote(meta.at[rows(src)], meta.at[rows(dst)], m_ss, m_rs.at[dst - 1], device).start()

    def hop(a, src, dst, k, device):
        cols = pl.ds(*HEAD[k])
        block = (xb, gb, xf)[a].at[:, cols] if src == 0 else ag.at[a, rows(src), cols]
        remote(block, ag.at[a, rows(dst), cols], z_ss.at[a], z_rs.at[a, dst - 1, k], device).start()

    def landed(a, block, k):
        take(ag.at[a, rows(block), pl.ds(*HEAD[k])], z_rs.at[a, block - 1, k], behind)

    def first_hops(a):
        for k in range(NH):
            hop(a, 0, 1, k, ahead)
            hop(a, 0, 7, k, behind)

    def forward_hops(a, with_meta=False):
        for s in (1, 2, 3):
            if with_meta:
                take(meta.at[rows(s)], m_rs.at[s - 1], behind)
                meta_hop(s, s + 1, ahead)
                take(meta.at[rows(8 - s)], m_rs.at[7 - s], ahead)
                if s < 3:
                    meta_hop(8 - s, 7 - s, behind)
            for k in range(NH):
                landed(a, s, k)
                hop(a, s, s + 1, k, ahead)
                landed(a, 8 - s, k)
                if s < 3:
                    hop(a, 8 - s, 7 - s, k, behind)

    def build(which):
        every = meta[...]
        lane = lax.broadcasted_iota(jnp.int32, (GROUP, 128), 1)
        base = 2 * E * (1 - which) + z * NY

        def column(off):
            return jnp.sum(jnp.where(lane == off, every, 0.0), axis=1, keepdims=True)

        r = lax.broadcasted_iota(jnp.int32, (GROUP, TILE), 1)
        t = lax.broadcasted_iota(jnp.int32, (GROUP, TILE), 0)
        j = jnp.zeros_like(r)
        for i in range(1, NY):
            j = j + jnp.where(r >= i * SLOT, 1, 0)
        r = r - j * SLOT
        source = jnp.zeros_like(r)
        for i in range(1, NZ):
            source = source + jnp.where(r >= i * CAP, 1, 0)
        slot = (r - source * CAP).astype(F32)
        pos = jnp.zeros((GROUP, TILE), F32)
        share = jnp.zeros((GROUP, TILE), F32)
        for i in range(NY):
            off = base + lax.rem(y + i, NY)
            pos = jnp.where(j == i, column(off), pos)
            share = jnp.where(j == i, column(off + E), share)
        match = jnp.logical_and(lax.shift_right_logical(t, 4) == source, pos == slot)
        onehot[which] = jnp.where(match, 1.0, 0.0).T[0:PLANE].astype(BF)
        share = jnp.where(match, share, 0.0)
        high = share.astype(BF)
        mix_hi[which] = high[:, 0:PLANE]
        mix_lo[which] = (share - high.astype(F32)).astype(BF)[:, 0:PLANE]

    def gather(a, k):
        which = 1 if a == F else 0
        cols = pl.ds(*HEAD[k])
        landed(a, 4, k)
        picked = dot(onehot[which], ag[a, :, cols]).astype(BF)
        recv[a, 0:SLOT, cols] = picked[0:SLOT]
        send[a, :, cols] = picked[SLOT:PLANE]

    def dispatch(a, k):
        cols = pl.ds(*HEAD[k])
        for i in range(1, NY):
            remote(
                send.at[a, pl.ds((i - 1) * SLOT, SLOT), cols],
                recv.at[a, pl.ds(i * SLOT, SLOT), cols],
                y_ss.at[a], y_rs.at[a, k], ups[i],
            ).start()

    def arrived(a, k):
        cols = pl.ds(*HEAD[k])
        take(recv.at[a, pl.ds(SLOT, PLANE - SLOT), cols], y_rs.at[a, k], ups[1])
        remote(
            recv.at[a, pl.ds(0, PLANE), cols], recv.at[a, pl.ds(PLANE, PLANE), cols],
            d_ss.at[a], d_rs.at[a, k], sibling,
        ).start()

    def complete(a):
        for k in range(NH):
            take(recv.at[a, pl.ds(PLANE, PLANE), pl.ds(*HEAD[k])], d_rs.at[a, k], sibling)

    for k in (0,):
        meta_hop(0, 1, ahead)
        meta_hop(0, 7, behind)
    first_hops(X)
    ag[X, 0:TOK, :] = xb[...]
    ag[G, 0:TOK, :] = gb[...]
    ag[F, 0:TOK, :] = xf[...]
    forward_hops(X, with_meta=True)
    first_hops(G)
    take(meta.at[rows(4)], m_rs.at[3], behind)
    build(0)
    for k in range(NH):
        gather(X, k)
        dispatch(X, k)
    forward_hops(G)
    first_hops(F)
    for k in range(NH):
        gather(G, k)
        dispatch(G, k)
    build(1)
    forward_hops(F)
    for k in range(NH):
        gather(F, k)

    for copy in weight_copies:
        copy.wait()
    for k in range(NH):
        arrived(X, k)
    complete(X)

    def tile(n):
        return pl.ds(pl.multiple_of(n * TILE, TILE), TILE)

    def project(a):
        def step(n, carry):
            gate[:, tile(n)] = dot(recv[a], wg[:, tile(n)])
            up[:, tile(n)] = dot(recv[a], wu[:, tile(n)])
            return carry

        lax.fori_loop(0, FF // TILE, step, 0)

    project(X)
    for k in range(NH):
        arrived(G, k)
        dispatch(F, k)
    complete(G)

    def backward(n, carry):
        grad = dot_nt(recv[G], wd[tile(n), :])
        value = gate[:, tile(n)]
        sigma = jax.nn.sigmoid(value)
        hid_a[:, tile(n)] = (grad * up[:, tile(n)] * sigma * (1.0 + value * (1.0 - sigma))).astype(BF)
        hid_b[:, tile(n)] = (grad * value * sigma).astype(BF)
        return carry

    lax.fori_loop(0, FF // TILE, backward, 0)

    def halves(a, k, product):
        first, width = TAIL[k]

        def step(n, carry):
            both = product(tile(n))
            own[a, :, tile(n)] = both[0:PLANE]
            sib_s[a, :, tile(n)] = both[PLANE:ROWS].astype(BF)
            return carry

        lax.fori_loop(first // TILE, (first + width) // TILE, step, 0)
        cols = pl.ds(first, width)
        remote(sib_s.at[a, :, cols], sib_r.at[a, :, cols], p_ss.at[a], p_rs.at[a, k], sibling).start()

    def give_back(a, k):
        cols = pl.ds(*TAIL[k])
        take(sib_r.at[a, :, cols], p_rs.at[a, k], sibling)
        total = (own[a, :, cols] + sib_r[a, :, cols].astype(F32)).astype(BF)
        ret_r[a, 0:SLOT, cols] = total[0:SLOT]
        ret_s[a, :, cols] = total[SLOT:PLANE]
        for i in range(1, NY):
            remote(
                ret_s.at[a, pl.ds((i - 1) * SLOT, SLOT), cols],
                ret_r.at[a, pl.ds(i * SLOT, SLOT), cols],
                r_ss.at[a], r_rs.at[a, k], downs[i],
            ).start()

    def results(a, product):
        for k in range(NT):
            halves(a, k, product)
            if k > 0:
                give_back(a, k - 1)
        give_back(a, NT - 1)

    results(B, lambda t: dot_nt(hid_a[...], wg[t, :]) + dot_nt(hid_b[...], wu[t, :]))

    for k in range(NH):
        arrived(F, k)
    complete(F)
    project(F)

    def activate(n, carry):
        value = gate[:, tile(n)]
        hid_a[:, tile(n)] = (value * jax.nn.sigmoid(value) * up[:, tile(n)]).astype(BF)
        return carry

    lax.fori_loop(0, FF // TILE, activate, 0)
    results(O, lambda t: dot(hid_a[...], wd[:, t]))

    def mixed(a, k):
        cols = pl.ds(*TAIL[k])
        take(ret_r.at[a, pl.ds(SLOT, PLANE - SLOT), cols], r_rs.at[a, k], downs[1])
        value = ret_r[a, :, cols]
        part[a, :, cols] = dot(mix_hi[a], value) + dot(mix_lo[a], value)

    def pass_on(a, k, block, add):
        cols = pl.ds(*TAIL[k])
        value = part[a, rows(block), cols]
        if add:
            take(rs_r.at[a, rows(block - 1), cols], c_rs.at[a, block - 1, k], behind)
            value = value + rs_r[a, rows(block - 1), cols].astype(F32)
        rs_s[a, rows(block - 1), cols] = value.astype(BF)
        if block <= 4:
            slot, device = (block - 2 if block > 1 else 3), behind
        else:
            slot, device = (block if block < 7 else 4), ahead
        remote(
            rs_s.at[a, rows(block - 1), cols], rs_r.at[a, rows(slot), cols],
            c_ss.at[a], c_rs.at[a, slot, k], device,
        ).start()

    def reduce_step(a, k, s):
        cols = pl.ds(*TAIL[k])
        if s == 0:
            mixed(a, k)
        if s < 4:
            pass_on(a, k, 4 - s, s > 0)
        if s < 3:
            pass_on(a, k, 5 + s, s > 0)
        if s == 4:
            take(rs_r.at[a, rows(3), cols], c_rs.at[a, 3, k], behind)
            take(rs_r.at[a, rows(4), cols], c_rs.at[a, 4, k], ahead)
            value = part[a, rows(0), cols]
            value = value + rs_r[a, rows(3), cols].astype(F32) + rs_r[a, rows(4), cols].astype(F32)
            xs[a, :, cols] = value.astype(BF)
            remote(
                xs.at[a, :, cols], xr.at[a, :, cols], x_ss.at[a], x_rs.at[a, k],
                x_next if a == O else x_prev,
            ).start()

    items = [(a, k) for a in (B, O) for k in range(NT)]
    for tick in range(len(items) + 4):
        for i, (a, k) in enumerate(items):
            s = tick - i
            if 0 <= s <= 4:
                reduce_step(a, k, s)

    sent(meta.at[pl.ds(0, 7 * TOK)], m_ss, behind)
    for a in (X, G, F):
        sent(ag.at[a, pl.ds(0, 7 * TOK)], z_ss.at[a], behind)
        sent(send.at[a], y_ss.at[a], behind)
        sent(recv.at[a, pl.ds(0, PLANE)], d_ss.at[a], behind)
    for a in (B, O):
        sent(sib_s.at[a], p_ss.at[a], behind)
        sent(ret_s.at[a], r_ss.at[a], behind)
        sent(rs_s.at[a], c_ss.at[a], behind)
    for a, out, empty in ((B, out_b, NX - 1), (O, out_f, 0)):
        for k in range(NT):
            take(xr.at[a, :, pl.ds(*TAIL[k])], x_rs.at[a, k], behind)
        out[...] = jnp.where(px == empty, jnp.zeros_like(out), xr[a])
        sent(xs.at[a], x_ss.at[a], behind)


def local(
    fwd_input, fwd_routes, fwd_weight, bwd_input, bwd_grad, bwd_routes, bwd_weight, w_gate, w_up, w_down
):
    vmem = pl.BlockSpec(memory_space=pltpu.VMEM)
    hbm = pl.BlockSpec(memory_space=pl.ANY)
    dma = pltpu.SemaphoreType.DMA
    out = jax.ShapeDtypeStruct((TOK, D), BF)
    fwd_next, grad_prev = pl.pallas_call(
        kernel,
        out_shape=(out, out),
        in_specs=[vmem] * 7 + [hbm] * 3,
        out_specs=(vmem, vmem),
        scratch_shapes=[
            pltpu.VMEM((D, FF), BF),
            pltpu.VMEM((D, FF), BF),
            pltpu.VMEM((FF, D), BF),
            pltpu.VMEM((GROUP, 128), F32),
            pltpu.VMEM((2, PLANE, GROUP), BF),
            pltpu.VMEM((2, GROUP, PLANE), BF),
            pltpu.VMEM((2, GROUP, PLANE), BF),
            pltpu.VMEM((3, GROUP, D), BF),
            pltpu.VMEM((3, PLANE - SLOT, D), BF),
            pltpu.VMEM((3, ROWS, D), BF),
            pltpu.VMEM((ROWS, FF), F32),
            pltpu.VMEM((ROWS, FF), F32),
            pltpu.VMEM((ROWS, FF), BF),
            pltpu.VMEM((ROWS, FF), BF),
            pltpu.VMEM((2, PLANE, D), F32),
            pltpu.VMEM((2, PLANE, D), BF),
            pltpu.VMEM((2, PLANE, D), BF),
            pltpu.VMEM((2, PLANE - SLOT, D), BF),
            pltpu.VMEM((2, PLANE, D), BF),
            pltpu.VMEM((2, GROUP, D), F32),
            pltpu.VMEM((2, 7 * TOK, D), BF),
            pltpu.VMEM((2, 7 * TOK, D), BF),
            pltpu.VMEM((2, TOK, D), BF),
            pltpu.VMEM((2, TOK, D), BF),
            dma((3,)),
            dma,
            dma((7,)),
            dma((3,)),
            dma((3, 7, NH)),
            dma((3,)),
            dma((3, NH)),
            dma((3,)),
            dma((3, NH)),
            dma((2,)),
            dma((2, NT)),
            dma((2,)),
            dma((2, NT)),
            dma((2,)),
            dma((2, 7, NT)),
            dma((2,)),
            dma((2, NT)),
        ],
        compiler_params=pltpu.CompilerParams(
            collective_id=0, has_side_effects=True, vmem_limit_bytes=60 * 2**20
        ),
        cost_estimate=pl.CostEstimate(
            flops=2 * 8 * ROWS * D * FF, bytes_accessed=3 * D * FF * 2, transcendentals=2 * ROWS * FF
        ),
    )(
        fwd_input[0], fwd_routes[0], fwd_weight[0], bwd_input[0], bwd_grad[0], bwd_routes[0], bwd_weight[0],
        w_gate[0, 0], w_up[0, 0], w_down[0, 0],
    )
    return fwd_next[None], grad_prev[None]


def solution(mesh):
    tokens = P("pipe", "expert", None)
    weights = P("pipe", "expert", None, None)
    return jax.shard_map(
        local,
        mesh=mesh,
        in_specs=(tokens,) * 7 + (weights,) * 3,
        out_specs=(tokens, tokens),
        check_vma=False,
    )
```

```python
import functools

import jax
import jax.numpy as jnp
from jax import lax
from jax.experimental import pallas as pl
from jax.experimental.pallas import tpu as pltpu
from jax.sharding import PartitionSpec as P

MESH = pl.DeviceIdType.MESH
BF = jnp.bfloat16
F32 = jnp.float32

D = 3584
FF = 512
TOK = 16
CAP = 6
E = 32
TOP = 8
NX = 4
NZ = 8
NY = 4
SLOT = NZ * CAP
PLANE = NY * SLOT
ROWS = 2 * PLANE
GROUP = NZ * TOK
TILE = 256

HEAD = ((0, 512), (512, 1024), (1536, 1024), (2560, 1024))
TAIL = ((0, 1024), (1024, 1024), (2048, 1024), (3072, 512))
NH = len(HEAD)
NT = len(TAIL)
X, G, F = 0, 1, 2
B, O = 0, 1


def dot(a, b):
    return jnp.dot(a, b, preferred_element_type=F32)


def dot_nt(a, b):
    return lax.dot_general(a, b, (((1,), (1,)), ((), ())), preferred_element_type=F32)


def slots_and_shares(routes, weights):
    expert = lax.broadcasted_iota(jnp.int32, (128, TOK), 0) & (E - 1)
    hit = jnp.zeros((128, TOK), F32)
    share = jnp.zeros((128, TOK), F32)
    for k in range(TOP):
        same = routes[k : k + 1, :] == expert
        hit = hit + jnp.where(same, 1.0, 0.0)
        share = share + jnp.where(same, weights[k : k + 1, :], 0.0)
    rows = lax.broadcasted_iota(jnp.int32, (TOK, TOK), 0)
    cols = lax.broadcasted_iota(jnp.int32, (TOK, TOK), 1)
    before = dot(hit.astype(BF), jnp.where(rows < cols, 1.0, 0.0).astype(BF))
    return jnp.where(hit > 0.5, before, -1.0), share


def kernel(
    xf, rf, wf, xb, gb, rb, wb, wg_h, wu_h, wd_h,
    out_f, out_b,
    wg, wu, wd, turned, meta, onehot, mix_hi, mix_lo, ag, send, recv,
    gate, up, hid_a, hid_b, own, sib_s, sib_r, ret_s, ret_r, part, rs_s, rs_r, xs, xr,
    met, w_sem, m_ss, m_rs, z_ss, z_rs, y_ss, y_rs, d_ss, d_rs,
    p_ss, p_rs, r_ss, r_rs, c_ss, c_rs, x_ss, x_rs,
):
    px = lax.axis_index("pipe")
    e = lax.axis_index("expert")
    c = lax.rem(e, 2)
    y = lax.rem(lax.div(e, 2), NY)
    z = lax.div(e, 2 * NY)
    turn = 1 - 2 * c

    def at(qx, qz, qy, qc):
        return (lax.rem(qx + NX, NX), (lax.rem(qz + NZ, NZ) * NY + lax.rem(qy + NY, NY)) * 2 + qc)

    ahead = at(px, z + turn, y, c)
    behind = at(px, z - turn, y, c)
    ups = [None] + [at(px, z, y + i, c) for i in range(1, NY)]
    downs = [None] + [at(px, z, y - i, c) for i in range(1, NY)]
    sibling = at(px, z, y, 1 - c)
    x_next = at(px + 1, z, y, c)
    x_prev = at(px - 1, z, y, c)

    def remote(src, dst, ss, rs, device):
        return pltpu.make_async_remote_copy(
            src_ref=src, dst_ref=dst, send_sem=ss, recv_sem=rs, device_id=device, device_id_type=MESH
        )

    def take(ref, rs, device):
        remote(ref, ref, rs, rs, device).wait_recv()

    def sent(ref, ss, device):
        remote(ref, ref, ss, ss, device).wait_send()

    weight_copies = [
        pltpu.make_async_copy(a, b, w_sem.at[i])
        for i, (a, b) in enumerate(((wg_h, wg), (wu_h, wu), (wd_h, wd)))
    ]
    for copy in weight_copies:
        copy.start()

    barrier = pltpu.get_barrier_semaphore()
    partners = [ahead, behind, ups[1], ups[2], ups[3], x_next, x_prev]
    for device in partners:
        pl.semaphore_signal(barrier, inc=1, device_id=device, device_id_type=MESH)

    @pl.when(c == 0)
    def _():
        pl.semaphore_signal(barrier, inc=1, device_id=sibling, device_id_type=MESH)

    kind = lax.broadcasted_iota(jnp.int32, (128, TOK), 0)
    pos_f, share_f = slots_and_shares(rf[...], wf[...])
    pos_b, share_b = slots_and_shares(rb[...], wb[...])
    turned[:, 0:TOK] = jnp.where(
        kind < E, pos_f, jnp.where(kind < 2 * E, share_f, jnp.where(kind < 3 * E, pos_b, share_b))
    )
    meta[0:TOK, :] = turned[...].T[0:TOK]
    pl.semaphore_wait(barrier, len(partners) + c)

    @pl.when(c == 1)
    def _():
        pl.semaphore_signal(met, inc=1, device_id=sibling, device_id_type=MESH)

    def meet():
        @pl.when(c == 0)
        def _():
            pl.semaphore_wait(met, 1)

    def rows(block):
        return pl.ds(block * TOK, TOK)

    def meta_hop(src, dst, device):
        remote(meta.at[rows(src)], meta.at[rows(dst)], m_ss, m_rs.at[dst - 1], device).start()

    def hop(a, src, dst, k, device):
        cols = pl.ds(*HEAD[k])
        block = (xb, gb, xf)[a].at[:, cols] if src == 0 else ag.at[a, rows(src), cols]
        remote(block, ag.at[a, rows(dst), cols], z_ss.at[a], z_rs.at[a, dst - 1, k], device).start()

    def landed(a, block, k):
        take(ag.at[a, rows(block), pl.ds(*HEAD[k])], z_rs.at[a, block - 1, k], behind)

    def first_hops(a):
        for k in range(NH):
            hop(a, 0, 1, k, ahead)
            hop(a, 0, 7, k, behind)

    def forward_hops(a, with_meta=False):
        for s in (1, 2, 3):
            if with_meta:
                take(meta.at[rows(s)], m_rs.at[s - 1], behind)
                meta_hop(s, s + 1, ahead)
                take(meta.at[rows(8 - s)], m_rs.at[7 - s], ahead)
                if s < 3:
                    meta_hop(8 - s, 7 - s, behind)
            for k in range(NH):
                landed(a, s, k)
                hop(a, s, s + 1, k, ahead)
                landed(a, 8 - s, k)
                if s < 3:
                    hop(a, 8 - s, 7 - s, k, behind)

    def build(which):
        every = meta[...]
        lane = lax.broadcasted_iota(jnp.int32, (GROUP, 128), 1)
        base = 2 * E * (1 - which) + z * NY

        def column(off):
            return jnp.sum(jnp.where(lane == off, every, 0.0), axis=1, keepdims=True)

        r = lax.broadcasted_iota(jnp.int32, (GROUP, TILE), 1)
        t = lax.broadcasted_iota(jnp.int32, (GROUP, TILE), 0)
        j = jnp.zeros_like(r)
        for i in range(1, NY):
            j = j + jnp.where(r >= i * SLOT, 1, 0)
        r = r - j * SLOT
        source = jnp.zeros_like(r)
        for i in range(1, NZ):
            source = source + jnp.where(r >= i * CAP, 1, 0)
        slot = (r - source * CAP).astype(F32)
        pos = jnp.zeros((GROUP, TILE), F32)
        share = jnp.zeros((GROUP, TILE), F32)
        for i in range(NY):
            off = base + lax.rem(y + i, NY)
            pos = jnp.where(j == i, column(off), pos)
            share = jnp.where(j == i, column(off + E), share)
        match = jnp.logical_and(lax.shift_right_logical(t, 4) == source, pos == slot)
        onehot[which] = jnp.where(match, 1.0, 0.0).T[0:PLANE].astype(BF)
        share = jnp.where(match, share, 0.0)
        high = share.astype(BF)
        mix_hi[which] = high[:, 0:PLANE]
        mix_lo[which] = (share - high.astype(F32)).astype(BF)[:, 0:PLANE]

    def gather(a, k):
        which = 1 if a == F else 0
        cols = pl.ds(*HEAD[k])
        landed(a, 4, k)
        picked = dot(onehot[which], ag[a, :, cols]).astype(BF)
        recv[a, 0:SLOT, cols] = picked[0:SLOT]
        send[a, :, cols] = picked[SLOT:PLANE]

    def dispatch(a, k):
        cols = pl.ds(*HEAD[k])
        for i in range(1, NY):
            remote(
                send.at[a, pl.ds((i - 1) * SLOT, SLOT), cols],
                recv.at[a, pl.ds(i * SLOT, SLOT), cols],
                y_ss.at[a], y_rs.at[a, k], ups[i],
            ).start()

    def arrived(a, k):
        cols = pl.ds(*HEAD[k])
        take(recv.at[a, pl.ds(SLOT, PLANE - SLOT), cols], y_rs.at[a, k], ups[1])
        remote(
            recv.at[a, pl.ds(0, PLANE), cols], recv.at[a, pl.ds(PLANE, PLANE), cols],
            d_ss.at[a], d_rs.at[a, k], sibling,
        ).start()

    def complete(a):
        for k in range(NH):
            take(recv.at[a, pl.ds(PLANE, PLANE), pl.ds(*HEAD[k])], d_rs.at[a, k], sibling)

    meta_hop(0, 1, ahead)
    meta_hop(0, 7, behind)
    first_hops(X)
    ag[X, 0:TOK, :] = xb[...]
    ag[G, 0:TOK, :] = gb[...]
    ag[F, 0:TOK, :] = xf[...]
    forward_hops(X, with_meta=True)
    first_hops(G)
    take(meta.at[rows(4)], m_rs.at[3], behind)
    build(0)
    for k in range(NH):
        gather(X, k)
        dispatch(X, k)
    forward_hops(G)
    first_hops(F)
    for k in range(NH):
        gather(G, k)
        dispatch(G, k)
    build(1)
    forward_hops(F)
    for copy in weight_copies:
        copy.wait()
    meet()
    for k in range(NH):
        arrived(X, k)
    for k in range(NH):
        gather(F, k)
        dispatch(F, k)


    def tile(n):
        return pl.ds(pl.multiple_of(n * TILE, TILE), TILE)

    def project(a):
        def step(n, carry):
            gate[:, tile(n)] = dot(recv[a], wg[:, tile(n)])
            up[:, tile(n)] = dot(recv[a], wu[:, tile(n)])
            return carry

        lax.fori_loop(0, FF // TILE, step, 0)

    complete(X)
    project(X)
    for k in range(NH):
        arrived(G, k)
    complete(G)

    def backward(n, carry):
        grad = dot_nt(recv[G], wd[tile(n), :])
        value = gate[:, tile(n)]
        sigma = jax.nn.sigmoid(value)
        hid_a[:, tile(n)] = (grad * up[:, tile(n)] * sigma * (1.0 + value * (1.0 - sigma))).astype(BF)
        hid_b[:, tile(n)] = (grad * value * sigma).astype(BF)
        return carry

    lax.fori_loop(0, FF // TILE, backward, 0)

    def halves(a, k, product):
        first, width = TAIL[k]

        def step(n, carry):
            both = product(tile(n))
            own[a, :, tile(n)] = both[0:PLANE]
            sib_s[a, :, tile(n)] = both[PLANE:ROWS].astype(BF)
            return carry

        lax.fori_loop(first // TILE, (first + width) // TILE, step, 0)
        cols = pl.ds(first, width)
        remote(sib_s.at[a, :, cols], sib_r.at[a, :, cols], p_ss.at[a], p_rs.at[a, k], sibling).start()

    def give_back(a, k):
        cols = pl.ds(*TAIL[k])
        take(sib_r.at[a, :, cols], p_rs.at[a, k], sibling)
        total = (own[a, :, cols] + sib_r[a, :, cols].astype(F32)).astype(BF)
        ret_r[a, 0:SLOT, cols] = total[0:SLOT]
        ret_s[a, :, cols] = total[SLOT:PLANE]
        for i in range(1, NY):
            remote(
                ret_s.at[a, pl.ds((i - 1) * SLOT, SLOT), cols],
                ret_r.at[a, pl.ds(i * SLOT, SLOT), cols],
                r_ss.at[a], r_rs.at[a, k], downs[i],
            ).start()

    def results(a, product):
        for k in range(NT):
            halves(a, k, product)
            if k > 0:
                give_back(a, k - 1)
        give_back(a, NT - 1)

    results(B, lambda t: dot_nt(hid_a[...], wg[t, :]) + dot_nt(hid_b[...], wu[t, :]))

    for k in range(NH):
        arrived(F, k)
    complete(F)
    project(F)

    def activate(n, carry):
        value = gate[:, tile(n)]
        hid_a[:, tile(n)] = (value * jax.nn.sigmoid(value) * up[:, tile(n)]).astype(BF)
        return carry

    lax.fori_loop(0, FF // TILE, activate, 0)
    results(O, lambda t: dot(hid_a[...], wd[:, t]))

    def mixed(a, k):
        cols = pl.ds(*TAIL[k])
        take(ret_r.at[a, pl.ds(SLOT, PLANE - SLOT), cols], r_rs.at[a, k], downs[1])
        value = ret_r[a, :, cols]
        part[a, :, cols] = dot(mix_hi[a], value) + dot(mix_lo[a], value)

    def pass_on(a, k, block, add):
        cols = pl.ds(*TAIL[k])
        value = part[a, rows(block), cols]
        if add:
            take(rs_r.at[a, rows(block - 1), cols], c_rs.at[a, block - 1, k], behind)
            value = value + rs_r[a, rows(block - 1), cols].astype(F32)
        rs_s[a, rows(block - 1), cols] = value.astype(BF)
        if block <= 4:
            slot, device = (block - 2 if block > 1 else 3), behind
        else:
            slot, device = (block if block < 7 else 4), ahead
        remote(
            rs_s.at[a, rows(block - 1), cols], rs_r.at[a, rows(slot), cols],
            c_ss.at[a], c_rs.at[a, slot, k], device,
        ).start()

    def reduce_step(a, k, s):
        cols = pl.ds(*TAIL[k])
        if s == 0:
            mixed(a, k)
        if s < 4:
            pass_on(a, k, 4 - s, s > 0)
        if s < 3:
            pass_on(a, k, 5 + s, s > 0)
        if s == 4:
            take(rs_r.at[a, rows(3), cols], c_rs.at[a, 3, k], behind)
            take(rs_r.at[a, rows(4), cols], c_rs.at[a, 4, k], ahead)
            value = part[a, rows(0), cols]
            value = value + rs_r[a, rows(3), cols].astype(F32) + rs_r[a, rows(4), cols].astype(F32)
            xs[a, :, cols] = value.astype(BF)
            remote(
                xs.at[a, :, cols], xr.at[a, :, cols], x_ss.at[a], x_rs.at[a, k],
                x_next if a == O else x_prev,
            ).start()

    items = [(a, k) for a in (B, O) for k in range(NT)]
    for tick in range(len(items) + 4):
        for i, (a, k) in enumerate(items):
            s = tick - i
            if 0 <= s <= 4:
                reduce_step(a, k, s)

    sent(meta.at[pl.ds(0, 7 * TOK)], m_ss, behind)
    for a in (X, G, F):
        sent(ag.at[a, pl.ds(0, 7 * TOK)], z_ss.at[a], behind)
        sent(send.at[a], y_ss.at[a], behind)
        sent(recv.at[a, pl.ds(0, PLANE)], d_ss.at[a], behind)
    for a in (B, O):
        sent(sib_s.at[a], p_ss.at[a], behind)
        sent(ret_s.at[a], r_ss.at[a], behind)
        sent(rs_s.at[a], c_ss.at[a], behind)
    for a, out in ((B, out_b), (O, out_f)):
        for k in range(NT):
            take(xr.at[a, :, pl.ds(*TAIL[k])], x_rs.at[a, k], behind)
        out[...] = xr[a]
        sent(xs.at[a], x_ss.at[a], behind)


def local(
    fwd_input, fwd_routes, fwd_weight, bwd_input, bwd_grad, bwd_routes, bwd_weight, w_gate, w_up, w_down
):
    vmem = pl.BlockSpec(memory_space=pltpu.VMEM)
    hbm = pl.BlockSpec(memory_space=pl.ANY)
    dma = pltpu.SemaphoreType.DMA
    out = jax.ShapeDtypeStruct((TOK, D), BF)
    fwd_next, grad_prev = pl.pallas_call(
        kernel,
        out_shape=(out, out),
        in_specs=[vmem] * 7 + [hbm] * 3,
        out_specs=(vmem, vmem),
        scratch_shapes=[
            pltpu.VMEM((D, FF), BF),
            pltpu.VMEM((D, FF), BF),
            pltpu.VMEM((FF, D), BF),
            pltpu.VMEM((128, 128), F32),
            pltpu.VMEM((GROUP, 128), F32),
            pltpu.VMEM((2, PLANE, GROUP), BF),
            pltpu.VMEM((2, GROUP, PLANE), BF),
            pltpu.VMEM((2, GROUP, PLANE), BF),
            pltpu.VMEM((3, GROUP, D), BF),
            pltpu.VMEM((3, PLANE - SLOT, D), BF),
            pltpu.VMEM((3, ROWS, D), BF),
            pltpu.VMEM((ROWS, FF), F32),
            pltpu.VMEM((ROWS, FF), F32),
            pltpu.VMEM((ROWS, FF), BF),
            pltpu.VMEM((ROWS, FF), BF),
            pltpu.VMEM((2, PLANE, D), F32),
            pltpu.VMEM((2, PLANE, D), BF),
            pltpu.VMEM((2, PLANE, D), BF),
            pltpu.VMEM((2, PLANE - SLOT, D), BF),
            pltpu.VMEM((2, PLANE, D), BF),
            pltpu.VMEM((2, GROUP, D), F32),
            pltpu.VMEM((2, 7 * TOK, D), BF),
            pltpu.VMEM((2, 7 * TOK, D), BF),
            pltpu.VMEM((2, TOK, D), BF),
            pltpu.VMEM((2, TOK, D), BF),
            pltpu.SemaphoreType.REGULAR,
            dma((3,)),
            dma,
            dma((7,)),
            dma((3,)),
            dma((3, 7, NH)),
            dma((3,)),
            dma((3, NH)),
            dma((3,)),
            dma((3, NH)),
            dma((2,)),
            dma((2, NT)),
            dma((2,)),
            dma((2, NT)),
            dma((2,)),
            dma((2, 7, NT)),
            dma((2,)),
            dma((2, NT)),
        ],
        compiler_params=pltpu.CompilerParams(
            collective_id=0, has_side_effects=True, vmem_limit_bytes=60 * 2**20
        ),
        cost_estimate=pl.CostEstimate(
            flops=2 * 8 * ROWS * D * FF, bytes_accessed=3 * D * FF * 2, transcendentals=2 * ROWS * FF
        ),
    )(
        fwd_input[0], fwd_routes[0].T, fwd_weight[0].T, bwd_input[0], bwd_grad[0], bwd_routes[0].T, bwd_weight[0].T,
        w_gate[0, 0], w_up[0, 0], w_down[0, 0],
    )
    px = lax.axis_index("pipe")
    fwd_next = jnp.where(px == 0, jnp.zeros_like(fwd_next), fwd_next)
    grad_prev = jnp.where(px == NX - 1, jnp.zeros_like(grad_prev), grad_prev)
    return fwd_next[None], grad_prev[None]


def solution(mesh):
    tokens = P("pipe", "expert", None)
    weights = P("pipe", "expert", None, None)
    return jax.shard_map(
        local,
        mesh=mesh,
        in_specs=(tokens,) * 7 + (weights,) * 3,
        out_specs=(tokens, tokens),
        check_vma=False,
    )
```

```python
import functools

import jax
import jax.numpy as jnp
from jax import lax
from jax.experimental import pallas as pl
from jax.experimental.pallas import tpu as pltpu
from jax.sharding import PartitionSpec as P

MESH = pl.DeviceIdType.MESH
BF = jnp.bfloat16
F32 = jnp.float32

D = 3584
FF = 512
TOK = 16
CAP = 6
E = 32
TOP = 8
NX = 4
NZ = 8
NY = 4
SLOT = NZ * CAP
PLANE = NY * SLOT
ROWS = 2 * PLANE
GROUP = NZ * TOK
TILE = 256
WIDE = 512

HEAD = ((0, 512), (512, 1024), (1536, 1024), (2560, 1024))
TAIL = ((0, 1024), (1024, 1024), (2048, 1024), (3072, 512))
NH = len(HEAD)
NT = len(TAIL)
X, G, F = 0, 1, 2
B, O = 0, 1


def dot(a, b):
    return jnp.dot(a, b, preferred_element_type=F32)


def dot_nt(a, b):
    return lax.dot_general(a, b, (((1,), (1,)), ((), ())), preferred_element_type=F32)


def slots_and_shares(routes, weights):
    expert = lax.broadcasted_iota(jnp.int32, (128, TOK), 0) & (E - 1)
    hit = jnp.zeros((128, TOK), F32)
    share = jnp.zeros((128, TOK), F32)
    for k in range(TOP):
        same = routes[k : k + 1, :] == expert
        hit = hit + jnp.where(same, 1.0, 0.0)
        share = share + jnp.where(same, weights[k : k + 1, :], 0.0)
    rows = lax.broadcasted_iota(jnp.int32, (TOK, TOK), 0)
    cols = lax.broadcasted_iota(jnp.int32, (TOK, TOK), 1)
    before = dot(hit.astype(BF), jnp.where(rows < cols, 1.0, 0.0).astype(BF))
    return jnp.where(hit > 0.5, before, -1.0), share


def kernel(
    xf, rf, wf, xb, gb, rb, wb, wg_h, wu_h, wd_h,
    out_f, out_b,
    wg, wu, wd, turned, meta, onehot, mix_hi, mix_lo, ag, send, recv,
    gate, up, hid_a, hid_b, own, sib_s, sib_r, ret_s, ret_r, part, rs_s, rs_r, xs, xr,
    met, o_sem, w_sem, m_ss, m_rs, z_ss, z_rs, y_ss, y_rs, d_ss, d_rs,
    p_ss, p_rs, r_ss, r_rs, c_ss, c_rs, x_ss, x_rs,
):
    px = lax.axis_index("pipe")
    e = lax.axis_index("expert")
    c = lax.rem(e, 2)
    y = lax.rem(lax.div(e, 2), NY)
    z = lax.div(e, 2 * NY)
    turn = 1 - 2 * c

    def at(qx, qz, qy, qc):
        return (lax.rem(qx + NX, NX), (lax.rem(qz + NZ, NZ) * NY + lax.rem(qy + NY, NY)) * 2 + qc)

    ahead = at(px, z + turn, y, c)
    behind = at(px, z - turn, y, c)
    ahead2 = at(px, z + 2 * turn, y, c)
    behind2 = at(px, z - 2 * turn, y, c)
    ups = [None] + [at(px, z, y + i, c) for i in range(1, NY)]
    downs = [None] + [at(px, z, y - i, c) for i in range(1, NY)]
    sibling = at(px, z, y, 1 - c)
    x_next = at(px + 1, z, y, c)
    x_prev = at(px - 1, z, y, c)

    def remote(src, dst, ss, rs, device):
        return pltpu.make_async_remote_copy(
            src_ref=src, dst_ref=dst, send_sem=ss, recv_sem=rs, device_id=device, device_id_type=MESH
        )

    def take(ref, rs, device):
        remote(ref, ref, rs, rs, device).wait_recv()

    def sent(ref, ss, device):
        remote(ref, ref, ss, ss, device).wait_send()

    weight_copies = [
        pltpu.make_async_copy(a, b, w_sem.at[i])
        for i, (a, b) in enumerate(((wg_h, wg), (wu_h, wu), (wd_h, wd)))
    ]
    own_copies = [
        pltpu.make_async_copy(src, ag.at[a, pl.ds(0, TOK)], o_sem.at[a]) for a, src in ((X, xb), (G, gb), (F, xf))
    ]
    for copy in own_copies + weight_copies:
        copy.start()

    barrier = pltpu.get_barrier_semaphore()
    partners = [ahead, behind, ahead2, behind2, ups[1], ups[2], ups[3], x_next, x_prev]
    for device in partners:
        pl.semaphore_signal(barrier, inc=1, device_id=device, device_id_type=MESH)

    @pl.when(c == 0)
    def _():
        pl.semaphore_signal(barrier, inc=1, device_id=sibling, device_id_type=MESH)

    kind = lax.broadcasted_iota(jnp.int32, (128, TOK), 0)
    pos_f, share_f = slots_and_shares(rf[...], wf[...])
    pos_b, share_b = slots_and_shares(rb[...], wb[...])
    turned[:, 0:TOK] = jnp.where(
        kind < E, pos_f, jnp.where(kind < 2 * E, share_f, jnp.where(kind < 3 * E, pos_b, share_b))
    )
    meta[0:TOK, :] = turned[...].T[0:TOK]
    pl.semaphore_wait(barrier, len(partners) + c)

    @pl.when(c == 1)
    def _():
        pl.semaphore_signal(met, inc=1, device_id=sibling, device_id_type=MESH)

    def meet():
        @pl.when(c == 0)
        def _():
            pl.semaphore_wait(met, 1)

    def rows(block):
        return pl.ds(block * TOK, TOK)

    def meta_hop(src, dst, device):
        remote(meta.at[rows(src)], meta.at[rows(dst)], m_ss, m_rs.at[dst - 1], device).start()

    def meta_landed(block):
        take(meta.at[rows(block)], m_rs.at[block - 1], behind)

    def hop(a, src, dst, k, device):
        cols = pl.ds(*HEAD[k])
        block = (xb, gb, xf)[a].at[:, cols] if src == 0 else ag.at[a, rows(src), cols]
        remote(block, ag.at[a, rows(dst), cols], z_ss.at[a], z_rs.at[a, dst - 1, k], device).start()

    def landed(a, block, k):
        take(ag.at[a, rows(block), pl.ds(*HEAD[k])], z_rs.at[a, block - 1, k], behind)

    first = ((2, ahead2), (6, behind2), (1, ahead), (7, behind))
    second = ((2, 4, ahead2), (2, 3, ahead), (6, 5, behind))

    def first_hops(a, k):
        for dst, device in first:
            hop(a, 0, dst, k, device)

    def second_hops(a, k):
        landed(a, 2, k)
        landed(a, 6, k)
        for src, dst, device in second:
            hop(a, src, dst, k, device)

    def build(which):
        every = meta[...]
        lane = lax.broadcasted_iota(jnp.int32, (GROUP, 128), 1)
        base = 2 * E * (1 - which) + z * NY

        def column(off):
            return jnp.sum(jnp.where(lane == off, every, 0.0), axis=1, keepdims=True)

        r = lax.broadcasted_iota(jnp.int32, (GROUP, TILE), 1)
        t = lax.broadcasted_iota(jnp.int32, (GROUP, TILE), 0)
        j = jnp.zeros_like(r)
        for i in range(1, NY):
            j = j + jnp.where(r >= i * SLOT, 1, 0)
        r = r - j * SLOT
        source = jnp.zeros_like(r)
        for i in range(1, NZ):
            source = source + jnp.where(r >= i * CAP, 1, 0)
        slot = (r - source * CAP).astype(F32)
        pos = jnp.zeros((GROUP, TILE), F32)
        share = jnp.zeros((GROUP, TILE), F32)
        for i in range(NY):
            off = base + lax.rem(y + i, NY)
            pos = jnp.where(j == i, column(off), pos)
            share = jnp.where(j == i, column(off + E), share)
        match = jnp.logical_and(lax.shift_right_logical(t, 4) == source, pos == slot)
        onehot[which] = jnp.where(match, 1.0, 0.0).T[0:PLANE].astype(BF)
        share = jnp.where(match, share, 0.0)
        high = share.astype(BF)
        mix_hi[which] = high[:, 0:PLANE]
        mix_lo[which] = (share - high.astype(F32)).astype(BF)[:, 0:PLANE]

    def gather(a, k):
        which = 1 if a == F else 0
        cols = pl.ds(*HEAD[k])
        for block in (1, 7, 3, 5, 4):
            landed(a, block, k)
        picked = dot(onehot[which], ag[a, :, cols]).astype(BF)
        recv[a, 0:SLOT, cols] = picked[0:SLOT]
        send[a, :, cols] = picked[SLOT:PLANE]

    def dispatch(a, k):
        cols = pl.ds(*HEAD[k])
        for i in range(1, NY):
            remote(
                send.at[a, pl.ds((i - 1) * SLOT, SLOT), cols],
                recv.at[a, pl.ds(i * SLOT, SLOT), cols],
                y_ss.at[a], y_rs.at[a, k], ups[i],
            ).start()

    def arrived(a, k):
        cols = pl.ds(*HEAD[k])
        take(recv.at[a, pl.ds(SLOT, PLANE - SLOT), cols], y_rs.at[a, k], ups[1])
        remote(
            recv.at[a, pl.ds(0, PLANE), cols], recv.at[a, pl.ds(PLANE, PLANE), cols],
            d_ss.at[a], d_rs.at[a, k], sibling,
        ).start()

    def complete(a):
        for k in range(NH):
            take(recv.at[a, pl.ds(PLANE, PLANE), pl.ds(*HEAD[k])], d_rs.at[a, k], sibling)

    queue = [(a, k) for a in (X, G, F) for k in range(NH)]
    for dst, device in first:
        meta_hop(0, dst, device)
    first_hops(*queue[0])
    first_hops(*queue[1])
    meta_landed(2)
    meta_landed(6)
    for src, dst, device in second:
        meta_hop(src, dst, device)
    for i, item in enumerate(queue):
        second_hops(*item)
        if i + 2 < len(queue):
            first_hops(*queue[i + 2])
        if i == 0:
            for block in (1, 7, 3, 5, 4):
                meta_landed(block)
            build(0)
            for copy in own_copies:
                copy.wait()
        if i > 0:
            gather(*queue[i - 1])
            dispatch(*queue[i - 1])
        if i == NH:
            build(1)
    for copy in weight_copies:
        copy.wait()
    meet()
    for k in range(NH):
        arrived(X, k)
    gather(*queue[-1])
    dispatch(*queue[-1])

    def tile(n, width=TILE):
        return pl.ds(pl.multiple_of(n * width, width), width)

    def project(a):
        def step(n, carry):
            gate[:, tile(n)] = dot(recv[a], wg[:, tile(n)])
            up[:, tile(n)] = dot(recv[a], wu[:, tile(n)])
            return carry

        lax.fori_loop(0, FF // TILE, step, 0)

    complete(X)
    project(X)
    for k in range(NH):
        arrived(G, k)
    complete(G)

    def backward(n, carry):
        grad = dot_nt(recv[G], wd[tile(n), :])
        value = gate[:, tile(n)]
        sigma = jax.nn.sigmoid(value)
        hid_a[:, tile(n)] = (grad * up[:, tile(n)] * sigma * (1.0 + value * (1.0 - sigma))).astype(BF)
        hid_b[:, tile(n)] = (grad * value * sigma).astype(BF)
        return carry

    lax.fori_loop(0, FF // TILE, backward, 0)

    def halves(a, k, product):
        first, width = TAIL[k]

        def step(n, carry):
            both = product(tile(n, WIDE))
            own[a, :, tile(n, WIDE)] = both[0:PLANE]
            sib_s[a, :, tile(n, WIDE)] = both[PLANE:ROWS].astype(BF)
            return carry

        lax.fori_loop(first // WIDE, (first + width) // WIDE, step, 0)
        cols = pl.ds(first, width)
        remote(sib_s.at[a, :, cols], sib_r.at[a, :, cols], p_ss.at[a], p_rs.at[a, k], sibling).start()

    def give_back(a, k):
        cols = pl.ds(*TAIL[k])
        take(sib_r.at[a, :, cols], p_rs.at[a, k], sibling)
        total = (own[a, :, cols] + sib_r[a, :, cols].astype(F32)).astype(BF)
        ret_r[a, 0:SLOT, cols] = total[0:SLOT]
        ret_s[a, :, cols] = total[SLOT:PLANE]
        for i in range(1, NY):
            remote(
                ret_s.at[a, pl.ds((i - 1) * SLOT, SLOT), cols],
                ret_r.at[a, pl.ds(i * SLOT, SLOT), cols],
                r_ss.at[a], r_rs.at[a, k], downs[i],
            ).start()

    def results(a, product):
        for k in range(NT):
            halves(a, k, product)
            if k > 0:
                give_back(a, k - 1)
        give_back(a, NT - 1)

    results(B, lambda t: dot_nt(hid_a[...], wg[t, :]) + dot_nt(hid_b[...], wu[t, :]))

    for k in range(NH):
        arrived(F, k)
    complete(F)
    project(F)

    def activate(n, carry):
        value = gate[:, tile(n)]
        hid_a[:, tile(n)] = (value * jax.nn.sigmoid(value) * up[:, tile(n)]).astype(BF)
        return carry

    lax.fori_loop(0, FF // TILE, activate, 0)
    results(O, lambda t: dot(hid_a[...], wd[:, t]))

    def mixed(a, k):
        cols = pl.ds(*TAIL[k])
        take(ret_r.at[a, pl.ds(SLOT, PLANE - SLOT), cols], r_rs.at[a, k], downs[1])
        value = ret_r[a, :, cols]
        part[a, :, cols] = dot(mix_hi[a], value) + dot(mix_lo[a], value)

    def pass_on(a, k, block, device, add=()):
        cols = pl.ds(*TAIL[k])
        value = part[a, rows(block), cols]
        for other in add:
            take(rs_r.at[a, rows(other - 1), cols], c_rs.at[a, other - 1, k], behind)
            value = value + rs_r[a, rows(other - 1), cols].astype(F32)
        rs_s[a, rows(block - 1), cols] = value.astype(BF)
        remote(
            rs_s.at[a, rows(block - 1), cols], rs_r.at[a, rows(block - 1), cols],
            c_ss.at[a], c_rs.at[a, block - 1, k], device,
        ).start()

    def reduce_step(a, k, s):
        cols = pl.ds(*TAIL[k])
        if s == 0:
            mixed(a, k)
            pass_on(a, k, 4, behind2)
            pass_on(a, k, 5, ahead)
            pass_on(a, k, 3, behind)
            pass_on(a, k, 1, behind)
            pass_on(a, k, 7, ahead)
        if s == 1:
            pass_on(a, k, 6, ahead2, (5,))
            pass_on(a, k, 2, behind2, (3, 4))
        if s == 2:
            value = part[a, rows(0), cols]
            for block in (1, 7, 6, 2):
                take(rs_r.at[a, rows(block - 1), cols], c_rs.at[a, block - 1, k], behind)
                value = value + rs_r[a, rows(block - 1), cols].astype(F32)
            xs[a, :, cols] = value.astype(BF)
            remote(
                xs.at[a, :, cols], xr.at[a, :, cols], x_ss.at[a], x_rs.at[a, k],
                x_next if a == O else x_prev,
            ).start()

    items = [(a, k) for a in (B, O) for k in range(NT)]
    for tick in range(len(items) + 2):
        for s in range(3):
            if 0 <= tick - s < len(items):
                reduce_step(*items[tick - s], s)

    sent(meta.at[pl.ds(0, 7 * TOK)], m_ss, behind)
    for a in (X, G, F):
        sent(ag.at[a, pl.ds(0, 7 * TOK)], z_ss.at[a], behind)
        sent(send.at[a], y_ss.at[a], behind)
        sent(recv.at[a, pl.ds(0, PLANE)], d_ss.at[a], behind)
    for a in (B, O):
        sent(sib_s.at[a], p_ss.at[a], behind)
        sent(ret_s.at[a], r_ss.at[a], behind)
        sent(rs_s.at[a], c_ss.at[a], behind)
    for a, out in ((B, out_b), (O, out_f)):
        for k in range(NT):
            take(xr.at[a, :, pl.ds(*TAIL[k])], x_rs.at[a, k], behind)
        out[...] = xr[a]
        sent(xs.at[a], x_ss.at[a], behind)


def local(
    fwd_input, fwd_routes, fwd_weight, bwd_input, bwd_grad, bwd_routes, bwd_weight, w_gate, w_up, w_down
):
    vmem = pl.BlockSpec(memory_space=pltpu.VMEM)
    hbm = pl.BlockSpec(memory_space=pl.ANY)
    dma = pltpu.SemaphoreType.DMA
    out = jax.ShapeDtypeStruct((TOK, D), BF)
    fwd_next, grad_prev = pl.pallas_call(
        kernel,
        out_shape=(out, out),
        in_specs=[hbm, vmem, vmem, hbm, hbm, vmem, vmem, hbm, hbm, hbm],
        out_specs=(vmem, vmem),
        scratch_shapes=[
            pltpu.VMEM((D, FF), BF),
            pltpu.VMEM((D, FF), BF),
            pltpu.VMEM((FF, D), BF),
            pltpu.VMEM((128, 128), F32),
            pltpu.VMEM((GROUP, 128), F32),
            pltpu.VMEM((2, PLANE, GROUP), BF),
            pltpu.VMEM((2, GROUP, PLANE), BF),
            pltpu.VMEM((2, GROUP, PLANE), BF),
            pltpu.VMEM((3, GROUP, D), BF),
            pltpu.VMEM((3, PLANE - SLOT, D), BF),
            pltpu.VMEM((3, ROWS, D), BF),
            pltpu.VMEM((ROWS, FF), F32),
            pltpu.VMEM((ROWS, FF), F32),
            pltpu.VMEM((ROWS, FF), BF),
            pltpu.VMEM((ROWS, FF), BF),
            pltpu.VMEM((2, PLANE, D), F32),
            pltpu.VMEM((2, PLANE, D), BF),
            pltpu.VMEM((2, PLANE, D), BF),
            pltpu.VMEM((2, PLANE - SLOT, D), BF),
            pltpu.VMEM((2, PLANE, D), BF),
            pltpu.VMEM((2, GROUP, D), F32),
            pltpu.VMEM((2, 7 * TOK, D), BF),
            pltpu.VMEM((2, 7 * TOK, D), BF),
            pltpu.VMEM((2, TOK, D), BF),
            pltpu.VMEM((2, TOK, D), BF),
            pltpu.SemaphoreType.REGULAR,
            dma((3,)),
            dma((3,)),
            dma,
            dma((7,)),
            dma((3,)),
            dma((3, 7, NH)),
            dma((3,)),
            dma((3, NH)),
            dma((3,)),
            dma((3, NH)),
            dma((2,)),
            dma((2, NT)),
            dma((2,)),
            dma((2, NT)),
            dma((2,)),
            dma((2, 7, NT)),
            dma((2,)),
            dma((2, NT)),
        ],
        compiler_params=pltpu.CompilerParams(
            collective_id=0, has_side_effects=True, vmem_limit_bytes=60 * 2**20
        ),
        cost_estimate=pl.CostEstimate(
            flops=2 * 8 * ROWS * D * FF, bytes_accessed=3 * D * FF * 2, transcendentals=2 * ROWS * FF
        ),
    )(
        fwd_input[0], fwd_routes[0].T, fwd_weight[0].T, bwd_input[0], bwd_grad[0], bwd_routes[0].T, bwd_weight[0].T,
        w_gate[0, 0], w_up[0, 0], w_down[0, 0],
    )
    px = lax.axis_index("pipe")
    fwd_next = jnp.where(px == 0, jnp.zeros_like(fwd_next), fwd_next)
    grad_prev = jnp.where(px == NX - 1, jnp.zeros_like(grad_prev), grad_prev)
    return fwd_next[None], grad_prev[None]


def solution(mesh):
    tokens = P("pipe", "expert", None)
    weights = P("pipe", "expert", None, None)
    return jax.shard_map(
        local,
        mesh=mesh,
        in_specs=(tokens,) * 7 + (weights,) * 3,
        out_specs=(tokens, tokens),
        check_vma=False,
    )
```

```python
import functools

import jax
import jax.numpy as jnp
from jax import lax
from jax.experimental import pallas as pl
from jax.experimental.pallas import tpu as pltpu
from jax.sharding import PartitionSpec as P

MESH = pl.DeviceIdType.MESH
BF = jnp.bfloat16
F32 = jnp.float32

D = 3584
FF = 512
TOK = 16
CAP = 6
E = 32
TOP = 8
NX = 4
NZ = 8
NY = 4
SLOT = NZ * CAP
PLANE = NY * SLOT
ROWS = 2 * PLANE
GROUP = NZ * TOK
TILE = 256
WIDE = 512

HEAD = ((0, 512), (512, 1024), (1536, 1024), (2560, 1024))
TAIL = tuple((i * 512, 512) for i in range(7))
NH = len(HEAD)
NT = len(TAIL)
LAG = 3
X, G, F = 0, 1, 2
B, O = 0, 1


def dot(a, b):
    return jnp.dot(a, b, preferred_element_type=F32)


def dot_nt(a, b):
    return lax.dot_general(a, b, (((1,), (1,)), ((), ())), preferred_element_type=F32)


def slots_and_shares(routes, weights):
    expert = lax.broadcasted_iota(jnp.int32, (128, TOK), 0) & (E - 1)
    hit = jnp.zeros((128, TOK), F32)
    share = jnp.zeros((128, TOK), F32)
    for k in range(TOP):
        same = routes[k : k + 1, :] == expert
        hit = hit + jnp.where(same, 1.0, 0.0)
        share = share + jnp.where(same, weights[k : k + 1, :], 0.0)
    rows = lax.broadcasted_iota(jnp.int32, (TOK, TOK), 0)
    cols = lax.broadcasted_iota(jnp.int32, (TOK, TOK), 1)
    before = dot(hit.astype(BF), jnp.where(rows < cols, 1.0, 0.0).astype(BF))
    return jnp.where(hit > 0.5, before, -1.0), share


def kernel(
    xf, rf, wf, xb, gb, rb, wb, wg_h, wu_h, wd_h,
    out_f, out_b,
    wg, wu, wd, turned, meta, onehot, mix_hi, mix_lo, ag, send, recv,
    gate, up, hid_a, hid_b, own, sib_s, sib_r, ret_s, ret_r, part, rs_s, rs_r,
    met, o_sem, w_sem, m_ss, m_rs, z_ss, z_rs, y_ss, y_rs, d_ss, d_rs,
    p_ss, p_rs, r_ss, r_rs, c_ss, c_rs,
):
    px = lax.axis_index("pipe")
    e = lax.axis_index("expert")
    c = lax.rem(e, 2)
    y = lax.rem(lax.div(e, 2), NY)
    z = lax.div(e, 2 * NY)
    turn = 1 - 2 * c

    def at(qx, qz, qy, qc):
        return (lax.rem(qx + NX, NX), (lax.rem(qz + NZ, NZ) * NY + lax.rem(qy + NY, NY)) * 2 + qc)

    ahead = at(px, z + turn, y, c)
    behind = at(px, z - turn, y, c)
    ahead2 = at(px, z + 2 * turn, y, c)
    behind2 = at(px, z - 2 * turn, y, c)
    ups = [None] + [at(px, z, y + i, c) for i in range(1, NY)]
    downs = [None] + [at(px, z, y - i, c) for i in range(1, NY)]
    sibling = at(px, z, y, 1 - c)
    owners = [{i: at(px + step, z + i * turn, y, c) for i in (-2, -1, 0, 1, 2)} for step in (-1, 1)]

    def remote(src, dst, ss, rs, device):
        return pltpu.make_async_remote_copy(
            src_ref=src, dst_ref=dst, send_sem=ss, recv_sem=rs, device_id=device, device_id_type=MESH
        )

    def take(ref, rs, device):
        remote(ref, ref, rs, rs, device).wait_recv()

    def sent(ref, ss, device):
        remote(ref, ref, ss, ss, device).wait_send()

    weight_copies = [
        pltpu.make_async_copy(a, b, w_sem.at[i])
        for i, (a, b) in enumerate(((wg_h, wg), (wu_h, wu), (wd_h, wd)))
    ]
    own_copies = [
        pltpu.make_async_copy(src, ag.at[a, pl.ds(0, TOK)], o_sem.at[a]) for a, src in ((X, xb), (G, gb), (F, xf))
    ]
    for copy in own_copies + weight_copies:
        copy.start()

    barrier = pltpu.get_barrier_semaphore()
    partners = [ahead, behind, ahead2, behind2, ups[1], ups[2], ups[3], *owners[0].values(), *owners[1].values()]
    for device in partners:
        pl.semaphore_signal(barrier, inc=1, device_id=device, device_id_type=MESH)

    @pl.when(c == 0)
    def _():
        pl.semaphore_signal(barrier, inc=1, device_id=sibling, device_id_type=MESH)

    kind = lax.broadcasted_iota(jnp.int32, (128, TOK), 0)
    pos_f, share_f = slots_and_shares(rf[...], wf[...])
    pos_b, share_b = slots_and_shares(rb[...], wb[...])
    turned[:, 0:TOK] = jnp.where(
        kind < E, pos_f, jnp.where(kind < 2 * E, share_f, jnp.where(kind < 3 * E, pos_b, share_b))
    )
    meta[0:TOK, :] = turned[...].T[0:TOK]
    pl.semaphore_wait(barrier, len(partners) + c)

    @pl.when(c == 1)
    def _():
        pl.semaphore_signal(met, inc=1, device_id=sibling, device_id_type=MESH)

    def meet():
        @pl.when(c == 0)
        def _():
            pl.semaphore_wait(met, 1)

    def rows(block):
        return pl.ds(block * TOK, TOK)

    def meta_hop(src, dst, device):
        remote(meta.at[rows(src)], meta.at[rows(dst)], m_ss, m_rs.at[dst - 1], device).start()

    def meta_landed(block):
        take(meta.at[rows(block)], m_rs.at[block - 1], behind)

    def hop(a, src, dst, k, device):
        cols = pl.ds(*HEAD[k])
        block = (xb, gb, xf)[a].at[:, cols] if src == 0 else ag.at[a, rows(src), cols]
        remote(block, ag.at[a, rows(dst), cols], z_ss.at[a], z_rs.at[a, dst - 1, k], device).start()

    def landed(a, block, k):
        take(ag.at[a, rows(block), pl.ds(*HEAD[k])], z_rs.at[a, block - 1, k], behind)

    first = ((2, ahead2), (6, behind2), (1, ahead), (7, behind))
    second = ((2, 4, ahead2), (2, 3, ahead), (6, 5, behind))

    def first_hops(a, k):
        for dst, device in first:
            hop(a, 0, dst, k, device)

    def second_hops(a, k):
        landed(a, 2, k)
        landed(a, 6, k)
        for src, dst, device in second:
            hop(a, src, dst, k, device)

    def build(which):
        every = meta[...]
        lane = lax.broadcasted_iota(jnp.int32, (GROUP, 128), 1)
        base = 2 * E * (1 - which) + z * NY

        def column(off):
            return jnp.sum(jnp.where(lane == off, every, 0.0), axis=1, keepdims=True)

        r = lax.broadcasted_iota(jnp.int32, (GROUP, TILE), 1)
        t = lax.broadcasted_iota(jnp.int32, (GROUP, TILE), 0)
        j = jnp.zeros_like(r)
        for i in range(1, NY):
            j = j + jnp.where(r >= i * SLOT, 1, 0)
        r = r - j * SLOT
        source = jnp.zeros_like(r)
        for i in range(1, NZ):
            source = source + jnp.where(r >= i * CAP, 1, 0)
        slot = (r - source * CAP).astype(F32)
        pos = jnp.zeros((GROUP, TILE), F32)
        share = jnp.zeros((GROUP, TILE), F32)
        for i in range(NY):
            off = base + lax.rem(y + i, NY)
            pos = jnp.where(j == i, column(off), pos)
            share = jnp.where(j == i, column(off + E), share)
        match = jnp.logical_and(lax.shift_right_logical(t, 4) == source, pos == slot)
        onehot[which] = jnp.where(match, 1.0, 0.0).T[0:PLANE].astype(BF)
        share = jnp.where(match, share, 0.0)
        high = share.astype(BF)
        mix_hi[which] = high[:, 0:PLANE]
        mix_lo[which] = (share - high.astype(F32)).astype(BF)[:, 0:PLANE]

    def gather(a, k):
        which = 1 if a == F else 0
        cols = pl.ds(*HEAD[k])
        for block in (1, 7, 3, 5, 4):
            landed(a, block, k)
        picked = dot(onehot[which], ag[a, :, cols]).astype(BF)
        recv[a, 0:SLOT, cols] = picked[0:SLOT]
        send[a, :, cols] = picked[SLOT:PLANE]

    def dispatch(a, k):
        cols = pl.ds(*HEAD[k])
        for i in range(1, NY):
            remote(
                send.at[a, pl.ds((i - 1) * SLOT, SLOT), cols],
                recv.at[a, pl.ds(i * SLOT, SLOT), cols],
                y_ss.at[a], y_rs.at[a, k], ups[i],
            ).start()

    def arrived(a, k):
        cols = pl.ds(*HEAD[k])
        take(recv.at[a, pl.ds(SLOT, PLANE - SLOT), cols], y_rs.at[a, k], ups[1])
        remote(
            recv.at[a, pl.ds(0, PLANE), cols], recv.at[a, pl.ds(PLANE, PLANE), cols],
            d_ss.at[a], d_rs.at[a, k], sibling,
        ).start()

    def complete(a):
        for k in range(NH):
            take(recv.at[a, pl.ds(PLANE, PLANE), pl.ds(*HEAD[k])], d_rs.at[a, k], sibling)

    queue = [(a, k) for a in (X, G, F) for k in range(NH)]
    for dst, device in first:
        meta_hop(0, dst, device)
    first_hops(*queue[0])
    first_hops(*queue[1])
    meta_landed(2)
    meta_landed(6)
    for src, dst, device in second:
        meta_hop(src, dst, device)
    for i, item in enumerate(queue):
        second_hops(*item)
        if i + 2 < len(queue):
            first_hops(*queue[i + 2])
        if i == 0:
            for block in (1, 7, 3, 5, 4):
                meta_landed(block)
            build(0)
            for copy in own_copies:
                copy.wait()
        if i in (1, 2):
            gather(*queue[i - 1])
            dispatch(*queue[i - 1])
        if i > 3:
            gather(*queue[i - 2])
            dispatch(*queue[i - 2])
        if i == NH:
            build(1)
    gather(*queue[-2])
    dispatch(*queue[-2])
    for copy in weight_copies:
        copy.wait()
    meet()
    for k in range(NH):
        arrived(X, k)
    gather(*queue[-1])
    dispatch(*queue[-1])

    def tile(n, width=TILE):
        return pl.ds(pl.multiple_of(n * width, width), width)

    def project(a):
        def step(n, carry):
            gate[:, tile(n)] = dot(recv[a], wg[:, tile(n)])
            up[:, tile(n)] = dot(recv[a], wu[:, tile(n)])
            return carry

        lax.fori_loop(0, FF // TILE, step, 0)

    complete(X)
    project(X)
    for k in range(NH):
        arrived(G, k)
    complete(G)

    def backward(n, carry):
        grad = dot_nt(recv[G], wd[tile(n), :])
        value = gate[:, tile(n)]
        sigma = jax.nn.sigmoid(value)
        hid_a[:, tile(n)] = (grad * up[:, tile(n)] * sigma * (1.0 + value * (1.0 - sigma))).astype(BF)
        hid_b[:, tile(n)] = (grad * value * sigma).astype(BF)
        return carry

    lax.fori_loop(0, FF // TILE, backward, 0)

    def halves(a, k, product):
        first, width = TAIL[k]

        def step(n, carry):
            both = product(tile(n, WIDE))
            own[a, :, tile(n, WIDE)] = both[0:PLANE]
            sib_s[a, :, tile(n, WIDE)] = both[PLANE:ROWS].astype(BF)
            return carry

        lax.fori_loop(first // WIDE, (first + width) // WIDE, step, 0)
        cols = pl.ds(first, width)
        remote(sib_s.at[a, :, cols], sib_r.at[a, :, cols], p_ss.at[a], p_rs.at[a, k], sibling).start()

    def give_back(a, k):
        cols = pl.ds(*TAIL[k])
        take(sib_r.at[a, :, cols], p_rs.at[a, k], sibling)
        total = (own[a, :, cols] + sib_r[a, :, cols].astype(F32)).astype(BF)
        ret_r[a, 0:SLOT, cols] = total[0:SLOT]
        ret_s[a, :, cols] = total[SLOT:PLANE]
        for i in range(1, NY):
            remote(
                ret_s.at[a, pl.ds((i - 1) * SLOT, SLOT), cols],
                ret_r.at[a, pl.ds(i * SLOT, SLOT), cols],
                r_ss.at[a], r_rs.at[a, k], downs[i],
            ).start()

    for k in range(NT):
        halves(B, k, lambda t: dot_nt(hid_a[...], wg[t, :]) + dot_nt(hid_b[...], wu[t, :]))
        if k > 0:
            give_back(B, k - 1)
    give_back(B, NT - 1)

    def mixed(a, k):
        cols = pl.ds(*TAIL[k])
        take(ret_r.at[a, pl.ds(SLOT, PLANE - SLOT), cols], r_rs.at[a, k], downs[1])
        value = ret_r[a, :, cols]
        part[a, :, cols] = dot(mix_hi[a], value) + dot(mix_lo[a], value)

    def pass_on(a, k, block, device, add=()):
        cols = pl.ds(*TAIL[k])
        value = part[a, rows(block), cols]
        for other in add:
            take(rs_r.at[a, rows(other), cols], c_rs.at[a, other, k], behind)
            value = value + rs_r[a, rows(other), cols].astype(F32)
        rs_s[a, rows(block), cols] = value.astype(BF)
        remote(
            rs_s.at[a, rows(block), cols], rs_r.at[a, rows(block), cols],
            c_ss.at[a], c_rs.at[a, block, k], device,
        ).start()

    def reduce_step(a, k, s):
        cols = pl.ds(*TAIL[k])
        if s == 0:
            mixed(a, k)
            pass_on(a, k, 4, behind2)
            pass_on(a, k, 5, ahead)
            pass_on(a, k, 3, behind)
            pass_on(a, k, 1, owners[a][-1])
            pass_on(a, k, 7, owners[a][1])
            pass_on(a, k, 0, owners[a][0])
        if s == 1:
            pass_on(a, k, 6, owners[a][2], (5,))
            pass_on(a, k, 2, owners[a][-2], (3, 4))
        if s == 2:
            value = jnp.zeros((TOK, TAIL[k][1]), F32)
            for block in (0, 1, 7, 6, 2):
                take(rs_r.at[a, rows(block), cols], c_rs.at[a, block, k], behind)
                value = value + rs_r[a, rows(block), cols].astype(F32)
            (out_b, out_f)[a][:, cols] = value.astype(BF)

    items = [(a, k) for a in (B, O) for k in range(NT)]

    def tick(t):
        for s in range(3):
            if 0 <= t - LAG * s < len(items):
                reduce_step(*items[t - LAG * s], s)

    for k in range(NH):
        arrived(F, k)
    complete(F)
    project(F)
    tick(0)

    def activate(n, carry):
        value = gate[:, tile(n)]
        hid_a[:, tile(n)] = (value * jax.nn.sigmoid(value) * up[:, tile(n)]).astype(BF)
        return carry

    lax.fori_loop(0, FF // TILE, activate, 0)
    for k in range(NT):
        halves(O, k, lambda t: dot(hid_a[...], wd[:, t]))
        if k > 0:
            give_back(O, k - 1)
            if k < NT - 1:
                tick(k)
    give_back(O, NT - 1)
    for t in range(NT - 1, len(items) + 2 * LAG):
        tick(t)

    sent(meta.at[pl.ds(0, 7 * TOK)], m_ss, behind)
    for a in (X, G, F):
        sent(ag.at[a, pl.ds(0, 7 * TOK)], z_ss.at[a], behind)
        sent(send.at[a], y_ss.at[a], behind)
        sent(recv.at[a, pl.ds(0, PLANE)], d_ss.at[a], behind)
    for a in (B, O):
        sent(sib_s.at[a], p_ss.at[a], behind)
        sent(ret_s.at[a], r_ss.at[a], behind)
        sent(rs_s.at[a], c_ss.at[a], behind)


def local(
    fwd_input, fwd_routes, fwd_weight, bwd_input, bwd_grad, bwd_routes, bwd_weight, w_gate, w_up, w_down
):
    vmem = pl.BlockSpec(memory_space=pltpu.VMEM)
    hbm = pl.BlockSpec(memory_space=pl.ANY)
    dma = pltpu.SemaphoreType.DMA
    out = jax.ShapeDtypeStruct((TOK, D), BF)
    fwd_next, grad_prev = pl.pallas_call(
        kernel,
        out_shape=(out, out),
        in_specs=[hbm, vmem, vmem, hbm, hbm, vmem, vmem, hbm, hbm, hbm],
        out_specs=(vmem, vmem),
        scratch_shapes=[
            pltpu.VMEM((D, FF), BF),
            pltpu.VMEM((D, FF), BF),
            pltpu.VMEM((FF, D), BF),
            pltpu.VMEM((128, 128), F32),
            pltpu.VMEM((GROUP, 128), F32),
            pltpu.VMEM((2, PLANE, GROUP), BF),
            pltpu.VMEM((2, GROUP, PLANE), BF),
            pltpu.VMEM((2, GROUP, PLANE), BF),
            pltpu.VMEM((3, GROUP, D), BF),
            pltpu.VMEM((3, PLANE - SLOT, D), BF),
            pltpu.VMEM((3, ROWS, D), BF),
            pltpu.VMEM((ROWS, FF), F32),
            pltpu.VMEM((ROWS, FF), F32),
            pltpu.VMEM((ROWS, FF), BF),
            pltpu.VMEM((ROWS, FF), BF),
            pltpu.VMEM((2, PLANE, D), F32),
            pltpu.VMEM((2, PLANE, D), BF),
            pltpu.VMEM((2, PLANE, D), BF),
            pltpu.VMEM((2, PLANE - SLOT, D), BF),
            pltpu.VMEM((2, PLANE, D), BF),
            pltpu.VMEM((2, GROUP, D), F32),
            pltpu.VMEM((2, GROUP, D), BF),
            pltpu.VMEM((2, GROUP, D), BF),
            pltpu.SemaphoreType.REGULAR,
            dma((3,)),
            dma((3,)),
            dma,
            dma((7,)),
            dma((3,)),
            dma((3, 7, NH)),
            dma((3,)),
            dma((3, NH)),
            dma((3,)),
            dma((3, NH)),
            dma((2,)),
            dma((2, NT)),
            dma((2,)),
            dma((2, NT)),
            dma((2,)),
            dma((2, 8, NT)),
        ],
        compiler_params=pltpu.CompilerParams(
            collective_id=0, has_side_effects=True, vmem_limit_bytes=60 * 2**20
        ),
        cost_estimate=pl.CostEstimate(
            flops=2 * 8 * ROWS * D * FF, bytes_accessed=3 * D * FF * 2, transcendentals=2 * ROWS * FF
        ),
    )(
        fwd_input[0], fwd_routes[0].T, fwd_weight[0].T, bwd_input[0], bwd_grad[0], bwd_routes[0].T, bwd_weight[0].T,
        w_gate[0, 0], w_up[0, 0], w_down[0, 0],
    )
    px = lax.axis_index("pipe")
    fwd_next = jnp.where(px == 0, jnp.zeros_like(fwd_next), fwd_next)
    grad_prev = jnp.where(px == NX - 1, jnp.zeros_like(grad_prev), grad_prev)
    return fwd_next[None], grad_prev[None]


def solution(mesh):
    tokens = P("pipe", "expert", None)
    weights = P("pipe", "expert", None, None)
    return jax.shard_map(
        local,
        mesh=mesh,
        in_specs=(tokens,) * 7 + (weights,) * 3,
        out_specs=(tokens, tokens),
        check_vma=False,
    )
```

```python
import functools

import jax
import jax.numpy as jnp
from jax import lax
from jax.experimental import pallas as pl
from jax.experimental.pallas import tpu as pltpu
from jax.sharding import PartitionSpec as P

MESH = pl.DeviceIdType.MESH
BF = jnp.bfloat16
F32 = jnp.float32

D = 3584
FF = 512
TOK = 16
CAP = 6
E = 32
TOP = 8
NX = 4
NZ = 8
NY = 4
SLOT = NZ * CAP
PLANE = NY * SLOT
ROWS = 2 * PLANE
GROUP = NZ * TOK
TILE = 256
WIDE = 512

HEAD = ((0, 512), (512, 1024), (1536, 1024), (2560, 1024))
TAIL = tuple((i * 512, 512) for i in range(7))
NH = len(HEAD)
NT = len(TAIL)
LAG = 3
X, G, F = 0, 1, 2
B, O = 0, 1


def dot(a, b):
    return jnp.dot(a, b, preferred_element_type=F32)


def dot_nt(a, b):
    return lax.dot_general(a, b, (((1,), (1,)), ((), ())), preferred_element_type=F32)


def slots_and_shares(routes, weights):
    expert = lax.broadcasted_iota(jnp.int32, (128, TOK), 0) & (E - 1)
    hit = jnp.zeros((128, TOK), F32)
    share = jnp.zeros((128, TOK), F32)
    for k in range(TOP):
        same = routes[k : k + 1, :] == expert
        hit = hit + jnp.where(same, 1.0, 0.0)
        share = share + jnp.where(same, weights[k : k + 1, :], 0.0)
    rows = lax.broadcasted_iota(jnp.int32, (TOK, TOK), 0)
    cols = lax.broadcasted_iota(jnp.int32, (TOK, TOK), 1)
    before = dot(hit.astype(BF), jnp.where(rows < cols, 1.0, 0.0).astype(BF))
    return jnp.where(hit > 0.5, before, -1.0), share


def kernel(
    xf, rf, wf, xb, gb, rb, wb, wg_h, wu_h, wd_h,
    out_f, out_b,
    wg, wu, wd, turned, meta, onehot, mix_hi, mix_lo, ag, send, recv,
    gate, up, hid_a, hid_b, own, sib_s, sib_r, ret_s, ret_r, part, rs_s, rs_r,
    met, o_sem, w_sem, m_ss, m_rs, z_ss, z_rs, y_ss, y_rs, d_ss, d_rs,
    p_ss, p_rs, r_ss, r_rs, c_ss, c_rs,
):
    px = lax.axis_index("pipe")
    e = lax.axis_index("expert")
    c = lax.rem(e, 2)
    y = lax.rem(lax.div(e, 2), NY)
    z = lax.div(e, 2 * NY)
    turn = 1 - 2 * c

    def at(qx, qz, qy, qc):
        return (lax.rem(qx + NX, NX), (lax.rem(qz + NZ, NZ) * NY + lax.rem(qy + NY, NY)) * 2 + qc)

    ahead = at(px, z + turn, y, c)
    behind = at(px, z - turn, y, c)
    ahead2 = at(px, z + 2 * turn, y, c)
    behind2 = at(px, z - 2 * turn, y, c)
    ups = [None] + [at(px, z, y + i, c) for i in range(1, NY)]
    downs = [None] + [at(px, z, y - i, c) for i in range(1, NY)]
    sibling = at(px, z, y, 1 - c)
    owners = [{i: at(px + step, z + i * turn, y, c) for i in (-2, -1, 0, 1, 2)} for step in (-1, 1)]

    def remote(src, dst, ss, rs, device):
        return pltpu.make_async_remote_copy(
            src_ref=src, dst_ref=dst, send_sem=ss, recv_sem=rs, device_id=device, device_id_type=MESH
        )

    def take(ref, rs, device):
        remote(ref, ref, rs, rs, device).wait_recv()

    def sent(ref, ss, device):
        remote(ref, ref, ss, ss, device).wait_send()

    weight_copies = [
        pltpu.make_async_copy(a, b, w_sem.at[i])
        for i, (a, b) in enumerate(((wg_h, wg), (wu_h, wu), (wd_h, wd)))
    ]
    own_copies = [
        pltpu.make_async_copy(src, ag.at[a, pl.ds(0, TOK)], o_sem.at[a]) for a, src in ((X, xb), (G, gb), (F, xf))
    ]
    for copy in own_copies + weight_copies:
        copy.start()

    barrier = pltpu.get_barrier_semaphore()
    partners = [ahead, behind, ahead2, behind2, ups[1], ups[2], ups[3], *owners[0].values(), *owners[1].values()]
    for device in partners:
        pl.semaphore_signal(barrier, inc=1, device_id=device, device_id_type=MESH)

    @pl.when(c == 0)
    def _():
        pl.semaphore_signal(barrier, inc=1, device_id=sibling, device_id_type=MESH)

    kind = lax.broadcasted_iota(jnp.int32, (128, TOK), 0)
    pos_f, share_f = slots_and_shares(rf[...], wf[...])
    pos_b, share_b = slots_and_shares(rb[...], wb[...])
    turned[:, 0:TOK] = jnp.where(
        kind < E, pos_f, jnp.where(kind < 2 * E, share_f, jnp.where(kind < 3 * E, pos_b, share_b))
    )
    meta[0:TOK, :] = turned[...].T[0:TOK]
    pl.semaphore_wait(barrier, len(partners) + c)

    @pl.when(c == 1)
    def _():
        pl.semaphore_signal(met, inc=1, device_id=sibling, device_id_type=MESH)

    def meet():
        @pl.when(c == 0)
        def _():
            pl.semaphore_wait(met, 1)

    def rows(block):
        return pl.ds(block * TOK, TOK)

    def meta_hop(src, dst, device):
        remote(meta.at[rows(src)], meta.at[rows(dst)], m_ss, m_rs.at[dst - 1], device).start()

    def meta_landed(block):
        take(meta.at[rows(block)], m_rs.at[block - 1], behind)

    def hop(a, src, dst, k, device):
        cols = pl.ds(*HEAD[k])
        block = (xb, gb, xf)[a].at[:, cols] if src == 0 else ag.at[a, rows(src), cols]
        remote(block, ag.at[a, rows(dst), cols], z_ss.at[a], z_rs.at[a, dst - 1, k], device).start()

    def landed(a, block, k):
        take(ag.at[a, rows(block), pl.ds(*HEAD[k])], z_rs.at[a, block - 1, k], behind)

    first = ((2, ahead2), (6, behind2), (1, ahead), (7, behind))
    second = ((2, 4, ahead2), (2, 3, ahead), (6, 5, behind))

    def first_hops(a, k):
        for dst, device in first:
            hop(a, 0, dst, k, device)

    def second_hops(a, k):
        landed(a, 2, k)
        landed(a, 6, k)
        for src, dst, device in second:
            hop(a, src, dst, k, device)

    def build(which):
        every = meta[...]
        lane = lax.broadcasted_iota(jnp.int32, (GROUP, 128), 1)
        base = 2 * E * (1 - which) + z * NY

        def column(off):
            return jnp.sum(jnp.where(lane == off, every, 0.0), axis=1, keepdims=True)

        r = lax.broadcasted_iota(jnp.int32, (GROUP, TILE), 1)
        t = lax.broadcasted_iota(jnp.int32, (GROUP, TILE), 0)
        j = jnp.zeros_like(r)
        for i in range(1, NY):
            j = j + jnp.where(r >= i * SLOT, 1, 0)
        r = r - j * SLOT
        source = jnp.zeros_like(r)
        for i in range(1, NZ):
            source = source + jnp.where(r >= i * CAP, 1, 0)
        slot = (r - source * CAP).astype(F32)
        pos = jnp.zeros((GROUP, TILE), F32)
        share = jnp.zeros((GROUP, TILE), F32)
        for i in range(NY):
            off = base + lax.rem(y + i, NY)
            pos = jnp.where(j == i, column(off), pos)
            share = jnp.where(j == i, column(off + E), share)
        match = jnp.logical_and(lax.shift_right_logical(t, 4) == source, pos == slot)
        onehot[which] = jnp.where(match, 1.0, 0.0).T[0:PLANE].astype(BF)
        share = jnp.where(match, share, 0.0)
        high = share.astype(BF)
        mix_hi[which] = high[:, 0:PLANE]
        mix_lo[which] = (share - high.astype(F32)).astype(BF)[:, 0:PLANE]

    def gather(a, k):
        which = 1 if a == F else 0
        cols = pl.ds(*HEAD[k])
        for block in (1, 7, 3, 5, 4):
            landed(a, block, k)
        picked = dot(onehot[which], ag[a, :, cols]).astype(BF)
        recv[a, 0:SLOT, cols] = picked[0:SLOT]
        send[a, :, cols] = picked[SLOT:PLANE]

    def dispatch(a, k):
        cols = pl.ds(*HEAD[k])
        for i in range(1, NY):
            remote(
                send.at[a, pl.ds((i - 1) * SLOT, SLOT), cols],
                recv.at[a, pl.ds(i * SLOT, SLOT), cols],
                y_ss.at[a], y_rs.at[a, k], ups[i],
            ).start()

    def arrived(a, k):
        cols = pl.ds(*HEAD[k])
        take(recv.at[a, pl.ds(SLOT, PLANE - SLOT), cols], y_rs.at[a, k], ups[1])
        remote(
            recv.at[a, pl.ds(0, PLANE), cols], recv.at[a, pl.ds(PLANE, PLANE), cols],
            d_ss.at[a], d_rs.at[a, k], sibling,
        ).start()

    def complete(a):
        for k in range(NH):
            take(recv.at[a, pl.ds(PLANE, PLANE), pl.ds(*HEAD[k])], d_rs.at[a, k], sibling)

    queue = [(a, k) for a in (X, G, F) for k in range(NH)]
    for dst, device in first:
        meta_hop(0, dst, device)
    first_hops(*queue[0])
    first_hops(*queue[1])
    meta_landed(2)
    meta_landed(6)
    for src, dst, device in second:
        meta_hop(src, dst, device)
    for i, item in enumerate(queue):
        second_hops(*item)
        if i + 2 < len(queue):
            first_hops(*queue[i + 2])
        if i == 0:
            for block in (1, 7, 3, 5, 4):
                meta_landed(block)
            build(0)
            for copy in own_copies:
                copy.wait()
        if i in (1, 2):
            gather(*queue[i - 1])
            dispatch(*queue[i - 1])
        if i > 3:
            gather(*queue[i - 2])
            dispatch(*queue[i - 2])
        if i == NH:
            build(1)
    gather(*queue[-2])
    dispatch(*queue[-2])
    for copy in weight_copies:
        copy.wait()
    meet()
    for k in range(NH):
        arrived(X, k)
    gather(*queue[-1])
    dispatch(*queue[-1])

    def tile(n, width=TILE):
        return pl.ds(pl.multiple_of(n * width, width), width)

    def project(a):
        def step(n, carry):
            gate[:, tile(n)] = dot(recv[a], wg[:, tile(n)])
            up[:, tile(n)] = dot(recv[a], wu[:, tile(n)])
            return carry

        lax.fori_loop(0, FF // TILE, step, 0)

    complete(X)
    project(X)
    for k in range(NH):
        arrived(G, k)
    complete(G)

    def backward(n, carry):
        grad = dot_nt(recv[G], wd[tile(n), :])
        value = gate[:, tile(n)]
        sigma = jax.nn.sigmoid(value)
        hid_a[:, tile(n)] = (grad * up[:, tile(n)] * sigma * (1.0 + value * (1.0 - sigma))).astype(BF)
        hid_b[:, tile(n)] = (grad * value * sigma).astype(BF)
        return carry

    lax.fori_loop(0, FF // TILE, backward, 0)

    def halves(a, k, product):
        first, width = TAIL[k]

        def step(n, carry):
            both = product(tile(n, WIDE))
            own[a, :, tile(n, WIDE)] = both[0:PLANE]
            sib_s[a, :, tile(n, WIDE)] = both[PLANE:ROWS].astype(BF)
            return carry

        lax.fori_loop(first // WIDE, (first + width) // WIDE, step, 0)
        cols = pl.ds(first, width)
        remote(sib_s.at[a, :, cols], sib_r.at[a, :, cols], p_ss.at[a], p_rs.at[a, k], sibling).start()

    def give_back(a, k):
        cols = pl.ds(*TAIL[k])
        take(sib_r.at[a, :, cols], p_rs.at[a, k], sibling)
        total = (own[a, :, cols] + sib_r[a, :, cols].astype(F32)).astype(BF)
        ret_r[a, 0:SLOT, cols] = total[0:SLOT]
        ret_s[a, :, cols] = total[SLOT:PLANE]
        for i in range(1, NY):
            remote(
                ret_s.at[a, pl.ds((i - 1) * SLOT, SLOT), cols],
                ret_r.at[a, pl.ds(i * SLOT, SLOT), cols],
                r_ss.at[a], r_rs.at[a, k], downs[i],
            ).start()

    for k in range(NT):
        halves(B, k, lambda t: dot_nt(hid_a[...], wg[t, :]) + dot_nt(hid_b[...], wu[t, :]))
        if k > 0:
            give_back(B, k - 1)
    give_back(B, NT - 1)

    def mixed(a, k):
        cols = pl.ds(*TAIL[k])
        take(ret_r.at[a, pl.ds(SLOT, PLANE - SLOT), cols], r_rs.at[a, k], downs[1])
        value = ret_r[a, :, cols]
        part[a, :, cols] = dot(mix_hi[a], value) + dot(mix_lo[a], value)

    def pass_on(a, k, block, device, add=()):
        cols = pl.ds(*TAIL[k])
        value = part[a, rows(block), cols]
        for other in add:
            take(rs_r.at[a, rows(other), cols], c_rs.at[a, other, k], behind)
            value = value + rs_r[a, rows(other), cols].astype(F32)
        rs_s[a, rows(block), cols] = value.astype(BF)
        remote(
            rs_s.at[a, rows(block), cols], rs_r.at[a, rows(block), cols],
            c_ss.at[a], c_rs.at[a, block, k], device,
        ).start()

    def reduce_step(a, k, s):
        cols = pl.ds(*TAIL[k])
        if s == 0:
            mixed(a, k)
            pass_on(a, k, 4, behind2)
            pass_on(a, k, 5, ahead)
            pass_on(a, k, 3, behind)
            pass_on(a, k, 1, owners[a][-1])
            pass_on(a, k, 7, owners[a][1])
            pass_on(a, k, 0, owners[a][0])
        if s == 1:
            pass_on(a, k, 6, owners[a][2], (5,))
            pass_on(a, k, 2, owners[a][-2], (3, 4))
        if s == 2:
            value = jnp.zeros((TOK, TAIL[k][1]), F32)
            for block in (0, 1, 7, 6, 2):
                take(rs_r.at[a, rows(block), cols], c_rs.at[a, block, k], behind)
                value = value + rs_r[a, rows(block), cols].astype(F32)
            (out_b, out_f)[a][:, cols] = value.astype(BF)

    items = [(a, k) for a in (B, O) for k in range(NT)]

    def tick(t):
        for s in range(3):
            if 0 <= t - LAG * s < len(items):
                reduce_step(*items[t - LAG * s], s)

    for k in range(NH):
        arrived(F, k)
    complete(F)
    project(F)
    tick(0)

    def activate(n, carry):
        value = gate[:, tile(n)]
        hid_a[:, tile(n)] = (value * jax.nn.sigmoid(value) * up[:, tile(n)]).astype(BF)
        return carry

    lax.fori_loop(0, FF // TILE, activate, 0)
    for k in range(NT):
        halves(O, k, lambda t: dot(hid_a[...], wd[:, t]))
        if k > 0:
            give_back(O, k - 1)
            if k < NT - 1:
                tick(k)
    give_back(O, NT - 1)
    for t in range(NT - 1, len(items)):
        tick(t)
    for i in range(len(items) - LAG, len(items)):
        reduce_step(*items[i], 1)
    for i in range(len(items) - 2 * LAG, len(items)):
        reduce_step(*items[i], 2)

    sent(meta.at[pl.ds(0, 7 * TOK)], m_ss, behind)
    for a in (X, G, F):
        sent(ag.at[a, pl.ds(0, 7 * TOK)], z_ss.at[a], behind)
        sent(send.at[a], y_ss.at[a], behind)
        sent(recv.at[a, pl.ds(0, PLANE)], d_ss.at[a], behind)
    for a in (B, O):
        sent(sib_s.at[a], p_ss.at[a], behind)
        sent(ret_s.at[a], r_ss.at[a], behind)
        sent(rs_s.at[a], c_ss.at[a], behind)


def local(
    fwd_input, fwd_routes, fwd_weight, bwd_input, bwd_grad, bwd_routes, bwd_weight, w_gate, w_up, w_down
):
    vmem = pl.BlockSpec(memory_space=pltpu.VMEM)
    hbm = pl.BlockSpec(memory_space=pl.ANY)
    dma = pltpu.SemaphoreType.DMA
    out = jax.ShapeDtypeStruct((TOK, D), BF)
    fwd_next, grad_prev = pl.pallas_call(
        kernel,
        out_shape=(out, out),
        in_specs=[hbm, vmem, vmem, hbm, hbm, vmem, vmem, hbm, hbm, hbm],
        out_specs=(vmem, vmem),
        scratch_shapes=[
            pltpu.VMEM((D, FF), BF),
            pltpu.VMEM((D, FF), BF),
            pltpu.VMEM((FF, D), BF),
            pltpu.VMEM((128, 128), F32),
            pltpu.VMEM((GROUP, 128), F32),
            pltpu.VMEM((2, PLANE, GROUP), BF),
            pltpu.VMEM((2, GROUP, PLANE), BF),
            pltpu.VMEM((2, GROUP, PLANE), BF),
            pltpu.VMEM((3, GROUP, D), BF),
            pltpu.VMEM((3, PLANE - SLOT, D), BF),
            pltpu.VMEM((3, ROWS, D), BF),
            pltpu.VMEM((ROWS, FF), F32),
            pltpu.VMEM((ROWS, FF), F32),
            pltpu.VMEM((ROWS, FF), BF),
            pltpu.VMEM((ROWS, FF), BF),
            pltpu.VMEM((2, PLANE, D), F32),
            pltpu.VMEM((2, PLANE, D), BF),
            pltpu.VMEM((2, PLANE, D), BF),
            pltpu.VMEM((2, PLANE - SLOT, D), BF),
            pltpu.VMEM((2, PLANE, D), BF),
            pltpu.VMEM((2, GROUP, D), F32),
            pltpu.VMEM((2, GROUP, D), BF),
            pltpu.VMEM((2, GROUP, D), BF),
            pltpu.SemaphoreType.REGULAR,
            dma((3,)),
            dma((3,)),
            dma,
            dma((7,)),
            dma((3,)),
            dma((3, 7, NH)),
            dma((3,)),
            dma((3, NH)),
            dma((3,)),
            dma((3, NH)),
            dma((2,)),
            dma((2, NT)),
            dma((2,)),
            dma((2, NT)),
            dma((2,)),
            dma((2, 8, NT)),
        ],
        compiler_params=pltpu.CompilerParams(
            collective_id=0, has_side_effects=True, vmem_limit_bytes=60 * 2**20
        ),
        cost_estimate=pl.CostEstimate(
            flops=2 * 8 * ROWS * D * FF, bytes_accessed=3 * D * FF * 2, transcendentals=2 * ROWS * FF
        ),
    )(
        fwd_input[0], fwd_routes[0].T, fwd_weight[0].T, bwd_input[0], bwd_grad[0], bwd_routes[0].T, bwd_weight[0].T,
        w_gate[0, 0], w_up[0, 0], w_down[0, 0],
    )
    px = lax.axis_index("pipe")
    fwd_next = jnp.where(px == 0, jnp.zeros_like(fwd_next), fwd_next)
    grad_prev = jnp.where(px == NX - 1, jnp.zeros_like(grad_prev), grad_prev)
    return fwd_next[None], grad_prev[None]


def solution(mesh):
    tokens = P("pipe", "expert", None)
    weights = P("pipe", "expert", None, None)
    return jax.shard_map(
        local,
        mesh=mesh,
        in_specs=(tokens,) * 7 + (weights,) * 3,
        out_specs=(tokens, tokens),
        check_vma=False,
    )
```
